256 devices in a mesh: row: 32 (over x, y, core), col: 8 (over z).
Axes of the slice: x: 4, y: 4, z: 8, core: 2. Of those that a mesh axis runs over, the one named last changes fastest.
Arguments:
- eigvec_rows: bfloat16 [16384, 65536], P('row', 'col'), may hold values from -6 to 6
- split: int32 [2], replicated, may hold values from 0 to 8191
- shifts: float32 [2, 65536], P(None, 'col'), as said below
- roots: float32 [128], replicated, as said below
- deflate_mask: int32 [2, 65536], P(None, 'col'), may hold values from 0 to 1
- panel_source: int32 [128], replicated, may hold values from 0 to 131071, as said below
Outputs:
- panel: float32 [128, 16384], P('col', 'row')
The draws below stay inside these ranges and needn't reach their ends.
Inputs may be any that keep to these rules, and one draw needn't show every extreme that they name: `shifts`: eigenvalues lie at least 0.02 from every secular root. `roots`: each root lies within 0.1 of an integer plus one half. `panel_source`: distinct indices; some are deflated and some are not.
All inputs are finite; a program needn't handle non-finite values.
Results may differ from the reference program's by a relative error of at most 0.002.
Values may be sent and summed in bfloat16 or wider, within the bound.
No kernel may reach another device: no remote copies, remote signals or barrier semaphores. Data moves between devices by JAX's collectives and lax.ppermute only.
A program may use at most 64 MiB of HBM per device.

```python
import jax
import jax.numpy as jnp
from jax import lax

HALF = 65536
PANEL = 128
WROWS = 8192


def deflation_plan(key):
    plan_key = jax.random.fold_in(key, 5)
    order_key, picks_key = jax.random.split(plan_key)
    order = jax.random.permutation(order_key, 2 * HALF)
    picks = jax.random.permutation(picks_key, 2 * (2 * HALF // 8))[:PANEL]
    return (order, picks)


def draw_shifts(key, part):
    key = jax.random.fold_in(key, 11)
    grid_key, offset_key = jax.random.split(key)
    grid = jax.random.randint(grid_key, (2, HALF), 0, 4096).astype(jnp.float32)
    offset = 0.3 * jnp.tanh(jax.random.normal(offset_key, (2, HALF), jnp.float32))
    return grid + offset


def draw_roots(key, part):
    key = jax.random.fold_in(key, 17)
    grid_key, offset_key = jax.random.split(key)
    grid = jax.random.randint(grid_key, (PANEL,), 0, 4096).astype(jnp.float32)
    offset = jax.random.uniform(offset_key, (PANEL,), jnp.float32, -0.1, 0.1)
    return grid + 0.5 + offset


def draw_deflate_mask(key, part):
    order, picks = deflation_plan(key)
    count = 2 * HALF // 8
    flat = jnp.zeros((2 * HALF,), jnp.int32).at[order[:count]].set(1)
    return flat.reshape(2, HALF)


def draw_panel_source(key, part):
    order, picks = deflation_plan(key)
    return order[picks].astype(jnp.int32)


def shard_levels(key, dims, pieces, low, high):
    factor_of = 1.0
    for dim, shards_of in pieces:
        heights = jax.random.uniform(jax.random.fold_in(jax.random.fold_in(key, 6), dim), (shards_of,), jnp.float32, low / len(pieces), high / len(pieces))
        factor_of = factor_of * jnp.repeat(jnp.exp(heights), dims[dim] // shards_of).reshape((-1,) + (1,) * (len(dims) - 1 - dim))
    return factor_of


def bell_draw(stream_key, extent, deviation, most, pieces=(), kind=jnp.bfloat16):
    factor_of = shard_levels(stream_key, extent, pieces, -0.22, 0.18) if pieces else 1.0
    result = jax.random.normal(stream_key, extent, jnp.float32) * deviation * factor_of
    return jnp.minimum(jnp.maximum(result, -most), most).astype(kind)


def setup_inputs(seed: int = 0) -> dict:
    seeds = jax.random.split(jax.random.key(seed), 7)
    return {
        "eigvec_rows": bell_draw(seeds[0], (2 * WROWS, HALF), 1.0, 6.0, ((0, 32), (1, 8))),
        "split": jax.random.randint(seeds[1], (2,), 0, WROWS).astype(jnp.int32),
        "shifts": draw_shifts(jax.random.fold_in(seeds[6], 71), 0),
        "roots": draw_roots(jax.random.fold_in(seeds[6], 71), 0),
        "deflate_mask": draw_deflate_mask(jax.random.fold_in(seeds[6], 71), 0),
        "panel_source": draw_panel_source(jax.random.fold_in(seeds[6], 71), 0),
    }


def reference(eigvec_rows, split, shifts, roots, deflate_mask, panel_source):
    blocks = eigvec_rows.reshape(2, WROWS, HALF)
    first = lax.dynamic_index_in_dim(blocks[0], split[0].astype(jnp.int32), 0, keepdims=False)
    second = lax.dynamic_index_in_dim(blocks[1], split[1].astype(jnp.int32), 0, keepdims=False)
    coupling = jnp.stack([first, second]).astype(jnp.float32)
    kept = jnp.where(deflate_mask == 1, jnp.float32(0.0), coupling)
    cauchy = kept[:, :, None] / (shifts[:, :, None] - roots[None, None, :])
    norm2 = lax.optimization_barrier(jnp.sum(cauchy * cauchy, axis=(0, 1)))
    deflated = deflate_mask.reshape(-1)[panel_source] == 1
    flat_index = jnp.arange(2 * HALF, dtype=jnp.int32).reshape(2, HALF)
    unit_part = (flat_index[:, :, None] == panel_source[None, None, :]).astype(jnp.float32)
    merged = jnp.where(deflated[None, None, :], unit_part, cauchy / jnp.sqrt(norm2)[None, None, :]).astype(jnp.bfloat16)
    outputs = []
    for which in range(2):
        outputs.append(lax.dot_general(merged[which], blocks[which], (((0,), (1,)), ((), ())), preferred_element_type=jnp.float32))
    return jnp.concatenate(outputs, axis=1)
```

```python
import functools

import jax
import jax.numpy as jnp
from jax import lax
from jax.experimental import pallas as pl
from jax.experimental.pallas import tpu as pltpu
from jax.sharding import PartitionSpec as P

LANES = 128
PIECE = 512
ALIGN = 16


def pick_kernel(split_ref, rows_ref, out_ref, window, sem, *, height):
    half = lax.axis_index("row") // (lax.axis_size("row") // 2)
    row = split_ref[half] % height
    base = pl.multiple_of((row // ALIGN) * ALIGN, ALIGN)
    copy = pltpu.make_async_copy(rows_ref.at[pl.ds(base, ALIGN)], window, sem)
    copy.start()
    copy.wait()
    inner = lax.broadcasted_iota(jnp.int32, (ALIGN, PIECE), 0) == row - base
    pieces = []
    for start in range(0, window.shape[1], PIECE):
        block = window[:, pl.ds(start, PIECE)].astype(jnp.float32)
        pieces.append(jnp.sum(jnp.where(inner, block, 0.0), axis=0, keepdims=True))
    line = jnp.concatenate(pieces, axis=0).astype(out_ref.dtype)
    for target in range(out_ref.shape[0]):
        out_ref[target] = line


def spread(line):
    return jnp.broadcast_to(line, (LANES, line.shape[1])).T


def merge_kernel(
    split_ref, line_ref, shifts_ref, mask_ref, roots_ref, source_ref, split_out, sums_ref,
    mask_line, kept_line, shift_line, *, height, width, columns
):
    row = lax.axis_index("row")
    half = row // (lax.axis_size("row") // 2)
    col = lax.axis_index("col")
    panel = roots_ref.shape[1]
    holder = split_ref[half] // height
    own = lambda ref, at: jnp.where(half == 0, ref[0:1, at], ref[1:2, at])
    local = source_ref[...] - (half * columns + col * width)
    here = (local >= 0) & (local < width)
    local = jnp.where(here, local, -1)
    local_all = spread(local)
    lane = lax.broadcasted_iota(jnp.int32, (panel, LANES), 1)
    tiles = width // LANES

    line = line_ref[holder].astype(jnp.float32)
    for a in range(width // PIECE):
        at = slice(a * PIECE, (a + 1) * PIECE)
        mask = own(mask_ref, at)
        mask_line[:, at] = mask
        kept_line[:, at] = jnp.where(mask == 1, 0.0, line[a : a + 1])
        shift_line[:, at] = own(shifts_ref, at)

    def count(t, flags):
        mask = mask_line[:, pl.ds(pl.multiple_of(t * LANES, LANES), LANES)]
        return flags + jnp.where((local_all == lane + t * LANES) & (mask == 1), 1.0, 0.0)

    flags = lax.fori_loop(0, tiles, count, jnp.zeros((panel, LANES), jnp.float32), unroll=4)
    flag = jnp.sum(flags, axis=1, keepdims=True)
    roots_all = jnp.where(flag > 0.5, 3e38, spread(roots_ref[...]))
    unit_all = jnp.where(flag > 0.5, local_all, -1)

    def body(t, norm):
        at = pl.ds(pl.multiple_of(t * LANES, LANES), LANES)
        cauchy = kept_line[:, at] / (shift_line[:, at] - roots_all)
        value = jnp.where(unit_all == lane + t * LANES, 1.0, cauchy)
        high = value.astype(jnp.bfloat16)
        split_out[0:panel, at] = high
        split_out[panel : 2 * panel, at] = (value - high.astype(jnp.float32)).astype(jnp.bfloat16)
        return norm + cauchy * cauchy

    norm = lax.fori_loop(0, tiles, body, jnp.zeros((panel, LANES), jnp.float32), unroll=4)
    total = jnp.sum(norm, axis=1, keepdims=True)
    position = lax.broadcasted_iota(jnp.int32, (panel, LANES), 1)
    sums_ref[...] = jnp.where(position == 0, total, jnp.where(position == 1, flag, 0.0))


def product_kernel(split_in, rows_ref, sums_ref, other_ref, out_ref):
    panel = sums_ref.shape[0]
    groups, per_group, _ = out_ref.shape
    height = rows_ref.shape[0]
    both = lax.dot_general(
        split_in[...], rows_ref[...], (((1,), (1,)), ((), ())), preferred_element_type=jnp.float32
    )
    out = both[0:panel] + both[panel : 2 * panel]
    own = sums_ref[...]
    other = other_ref[...]
    lane = lax.broadcasted_iota(jnp.int32, own.shape, 1)
    extra = own + jnp.where(lane == 0, other, jnp.where(lane == 2, pltpu.roll(other, 1, 1), 0.0))
    out_ref[:, :, 0:height] = out.reshape(groups, per_group, height)
    out_ref[:, :, height:] = extra.reshape(groups, per_group, LANES)


def finish_kernel(parts_ref, out_ref):
    groups = parts_ref.shape[0]
    height = out_ref.shape[1]
    extra = parts_ref[:, :, height:]
    total = jnp.sum(extra, axis=0)
    norm2 = total[:, 0:1]
    deflated = total[:, 1:2] + total[:, 2:3] > 0.5
    scale = 1.0 / jnp.sqrt(norm2)
    result = jnp.zeros(out_ref.shape, jnp.float32)
    for group in range(groups):
        weight = jnp.where(deflated, extra[group, :, 1:2], scale)
        result = result + weight * parts_ref[group, :, 0:height]
    out_ref[...] = jnp.where(deflated & (total[:, 1:2] < 0.5), 0.0, result)


def local(eigvec_rows, split, shifts, roots, deflate_mask, panel_source):
    height, width = eigvec_rows.shape
    row_count = lax.axis_size("row")
    col_count = lax.axis_size("col")
    half_devices = row_count // 2
    panel = roots.shape[0]
    vmem = pl.BlockSpec(memory_space=pltpu.VMEM)
    smem = pl.BlockSpec(memory_space=pltpu.SMEM)
    anywhere = pl.BlockSpec(memory_space=pl.ANY)
    lines = pl.pallas_call(
        functools.partial(pick_kernel, height=height),
        out_shape=jax.ShapeDtypeStruct((half_devices, width // PIECE, PIECE), eigvec_rows.dtype),
        in_specs=[smem, anywhere],
        out_specs=vmem,
        scratch_shapes=[pltpu.VMEM((ALIGN, width), eigvec_rows.dtype), pltpu.SemaphoreType.DMA],
        name="pick_line",
    )(split, eigvec_rows)
    halves = [list(range(half_devices)), list(range(half_devices, row_count))]
    lines = lax.all_to_all(lines, "row", 0, 0, axis_index_groups=halves)
    split_merged, sums = pl.pallas_call(
        functools.partial(merge_kernel, height=height, width=width, columns=width * col_count),
        out_shape=(
            jax.ShapeDtypeStruct((2 * panel, width), jnp.bfloat16),
            jax.ShapeDtypeStruct((panel, LANES), jnp.float32),
        ),
        in_specs=[smem, vmem, vmem, vmem, vmem, vmem],
        out_specs=(vmem, vmem),
        scratch_shapes=[pltpu.VMEM((1, width), kind) for kind in (jnp.int32, jnp.float32, jnp.float32)],
        compiler_params=pltpu.CompilerParams(vmem_limit_bytes=32 * 2**20),
        name="merge_columns",
    )(split, lines, shifts, deflate_mask, roots.reshape(1, -1), panel_source.reshape(1, -1))
    flip = half_devices + half_devices // 2
    other = lax.ppermute(sums, "row", [(i, i ^ flip) for i in range(row_count)])
    parts = pl.pallas_call(
        product_kernel,
        out_shape=jax.ShapeDtypeStruct((col_count, panel // col_count, height + LANES), jnp.float32),
        in_specs=[vmem, vmem, vmem, vmem],
        out_specs=vmem,
        compiler_params=pltpu.CompilerParams(vmem_limit_bytes=32 * 2**20),
        name="block_product",
    )(split_merged, eigvec_rows, sums, other)
    parts = lax.all_to_all(parts, "col", 0, 0)
    return pl.pallas_call(
        finish_kernel,
        out_shape=jax.ShapeDtypeStruct((panel // col_count, height), jnp.float32),
        in_specs=[vmem],
        out_specs=vmem,
        name="scale_and_add",
    )(parts)


def solution(mesh):
    return jax.shard_map(
        local,
        mesh=mesh,
        in_specs=(P("row", "col"), P(), P(None, "col"), P(), P(None, "col"), P()),
        out_specs=P("col", "row"),
        check_vma=False,
    )
```

```python
import functools

import jax
import jax.numpy as jnp
from jax import lax
from jax.experimental import pallas as pl
from jax.experimental.pallas import tpu as pltpu
from jax.sharding import PartitionSpec as P

LANES = 128
PIECE = 512
ALIGN = 16
SUBLANES = 8


def pick_kernel(split_ref, rows_ref, out_ref, window, sem, *, height):
    half = lax.axis_index("row") // (lax.axis_size("row") // 2)
    row = split_ref[half] % height
    base = pl.multiple_of((row // ALIGN) * ALIGN, ALIGN)
    copy = pltpu.make_async_copy(rows_ref.at[pl.ds(base, ALIGN)], window, sem)
    copy.start()
    copy.wait()
    inner = row - base
    lower = inner < SUBLANES
    inner = lax.rem(inner, SUBLANES)
    sublane = lax.broadcasted_iota(jnp.int32, (SUBLANES, PIECE), 0)
    blocks = [jnp.zeros((SUBLANES, PIECE), jnp.float32) for _ in range(out_ref.shape[1] // SUBLANES)]
    for a in range(out_ref.shape[1]):
        both = window[:, a * PIECE : (a + 1) * PIECE].astype(jnp.float32)
        eight = jnp.where(lower, both[0:SUBLANES], both[SUBLANES:])
        target = a % SUBLANES
        turned = pltpu.roll(eight, lax.rem(target - inner + SUBLANES, SUBLANES), 0)
        blocks[a // SUBLANES] = jnp.where(sublane == target, turned, blocks[a // SUBLANES])
    line = jnp.concatenate(blocks, axis=0).astype(out_ref.dtype)
    for target in range(out_ref.shape[0]):
        out_ref[target] = line


def held_kernel(split_ref, lines_ref, out_ref, *, height):
    half = lax.axis_index("row") // (lax.axis_size("row") // 2)
    out_ref[...] = lines_ref[split_ref[half] // height]


def spread(line):
    return jnp.broadcast_to(line, (LANES, line.shape[1])).T


def line_of(half, ref, at):
    return jnp.where(half == 0, ref[0:1, at], ref[1:2, at])


def poles(half, line, mask_ref, shifts_ref, kept_line, shift_line):
    for a in range(line.shape[0]):
        at = slice(a * PIECE, (a + 1) * PIECE)
        kept_line[:, at] = jnp.where(line_of(half, mask_ref, at) == 1, 0.0, line[a : a + 1])
        shift_line[:, at] = line_of(half, shifts_ref, at)


def cauchy_tile(kept_line, shift_line, roots_all, at):
    gap = shift_line[:, at] - roots_all
    rough = pl.reciprocal(gap, approx=True)
    return (kept_line[:, at] * rough) * (2.0 - gap * rough)


def merge_kernel(
    split_ref, lines_ref, rows_ref, shifts_ref, mask_ref, roots_ref, source_ref,
    split_out, part_ref, sums_ref,
    mask_square, kept_line, shift_line, *, height, width, columns
):
    row = lax.axis_index("row")
    half = row // (lax.axis_size("row") // 2)
    col = lax.axis_index("col")
    panel = roots_ref.shape[1]
    first = part_ref.shape[1]
    tiles = width // LANES
    for h in range(2):
        for t in range(tiles):
            at = slice(t * LANES, (t + 1) * LANES)
            mask_square[h * tiles + t : h * tiles + t + 1, :] = mask_ref[h : h + 1, at].astype(jnp.float32)
    source = spread(source_ref[...])
    source_half = (source >= columns).astype(jnp.int32)
    local = source - source_half * columns - col * width
    here = (local >= 0) & (local < width)
    lane = lax.broadcasted_iota(jnp.int32, (panel, LANES), 1)
    tile_of = jnp.where(here, source_half * tiles + local // LANES, -1)
    picked = jnp.dot(
        jnp.where(lane == tile_of, 1.0, 0.0).astype(jnp.bfloat16),
        mask_square[...].astype(jnp.bfloat16),
        preferred_element_type=jnp.float32,
    )
    deflated = jnp.sum(jnp.where(lane == local % LANES, picked, 0.0), axis=1, keepdims=True) > 0.5
    own_flag = deflated & (source_half == half)
    roots_all = jnp.where(own_flag, 3e38, spread(roots_ref[...]))
    unit_all = jnp.where(own_flag, local, -1)
    line = lines_ref[split_ref[half] // height].astype(jnp.float32)
    poles(half, line, mask_ref, shifts_ref, kept_line, shift_line)
    first_lane = lax.broadcasted_iota(jnp.int32, (1, LANES), 1)

    def fill(t, norm):
        at = pl.ds(pl.multiple_of(t * LANES, LANES), LANES)
        cauchy = cauchy_tile(kept_line, shift_line, roots_all, at)
        value = jnp.where(unit_all == first_lane + t * LANES, 1.0, cauchy)
        high = value.astype(jnp.bfloat16)
        split_out[0:panel, at] = high
        split_out[panel : 2 * panel, at] = (value - high.astype(jnp.float32)).astype(jnp.bfloat16)
        return norm + cauchy * cauchy

    norm = lax.fori_loop(0, tiles, fill, jnp.zeros((panel, LANES), jnp.float32), unroll=4)
    total = lax.dot_general(
        split_out[...], rows_ref[0:first], (((1,), (1,)), ((), ())), preferred_element_type=jnp.float32
    )
    part_ref[...] = total[0:panel] + total[panel : 2 * panel]
    norm = jnp.sum(norm, axis=1, keepdims=True)
    own = jnp.where(own_flag, 1.0, 0.0)
    other = jnp.where(deflated & (source_half != half), 1.0, 0.0)
    sums_ref[...] = jnp.where(lane == 0, norm, jnp.where(lane == 1, own, jnp.where(lane == 2, other, 0.0)))


def rest_kernel(
    other_ref, split_in, rows_ref, part_ref, sums_ref, shifts_ref, mask_ref, roots_ref,
    out_ref, kept_line, shift_line
):
    other_half = 1 - lax.axis_index("row") // (lax.axis_size("row") // 2)
    panel, first = part_ref.shape
    groups, per_group, _ = out_ref.shape
    height = rows_ref.shape[0]
    width = split_in.shape[1]
    poles(other_half, other_ref[...].astype(jnp.float32), mask_ref, shifts_ref, kept_line, shift_line)
    roots_all = spread(roots_ref[...])
    norm = jnp.zeros((panel, LANES), jnp.float32)
    total = jnp.zeros((2 * panel, height - first), jnp.float32)
    chunk = width // 8
    for c in range(8):
        at = slice(c * chunk, (c + 1) * chunk)
        total = total + lax.dot_general(
            split_in[:, at], rows_ref[first:, at], (((1,), (1,)), ((), ())), preferred_element_type=jnp.float32
        )
        for t in range(c * chunk // LANES, (c + 1) * chunk // LANES):
            cauchy = cauchy_tile(kept_line, shift_line, roots_all, slice(t * LANES, (t + 1) * LANES))
            norm = norm + cauchy * cauchy
    lane = lax.broadcasted_iota(jnp.int32, (panel, LANES), 1)
    extra = sums_ref[...] + jnp.where(lane == 0, jnp.sum(norm, axis=1, keepdims=True), 0.0)
    out_ref[:, :, 0:first] = part_ref[...].reshape(groups, per_group, first)
    out_ref[:, :, first:height] = (total[0:panel] + total[panel : 2 * panel]).reshape(groups, per_group, height - first)
    out_ref[:, :, height:] = extra.reshape(groups, per_group, LANES)


def finish_kernel(parts_ref, out_ref):
    groups = parts_ref.shape[0]
    height = out_ref.shape[1]
    extra = parts_ref[:, :, height:]
    total = jnp.sum(extra, axis=0)
    norm2 = total[:, 0:1]
    deflated = total[:, 1:2] + total[:, 2:3] > 0.5
    scale = 1.0 / jnp.sqrt(norm2)
    result = jnp.zeros(out_ref.shape, jnp.float32)
    for group in range(groups):
        weight = jnp.where(deflated, extra[group, :, 1:2], scale)
        result = result + weight * parts_ref[group, :, 0:height]
    out_ref[...] = jnp.where(deflated & (total[:, 1:2] < 0.5), 0.0, result)


def local(eigvec_rows, split, shifts, roots, deflate_mask, panel_source):
    height, width = eigvec_rows.shape
    row_count = lax.axis_size("row")
    col_count = lax.axis_size("col")
    half_devices = row_count // 2
    panel = roots.shape[0]
    first = height // 2
    lines_shape = (width // PIECE, PIECE)
    vmem = pl.BlockSpec(memory_space=pltpu.VMEM)
    smem = pl.BlockSpec(memory_space=pltpu.SMEM)
    anywhere = pl.BlockSpec(memory_space=pl.ANY)
    limit = lambda mib: pltpu.CompilerParams(vmem_limit_bytes=mib * 2**20)
    struct = jax.ShapeDtypeStruct
    roots = roots.reshape(1, -1)
    panel_source = panel_source.reshape(1, -1)
    lines = pl.pallas_call(
        functools.partial(pick_kernel, height=height),
        out_shape=struct((half_devices, *lines_shape), eigvec_rows.dtype),
        in_specs=[smem, anywhere],
        out_specs=vmem,
        scratch_shapes=[pltpu.VMEM((ALIGN, width), eigvec_rows.dtype), pltpu.SemaphoreType.DMA],
        compiler_params=limit(4),
        name="pick_line",
    )(pltpu.with_memory_space_constraint(split, pltpu.HBM), pltpu.with_memory_space_constraint(eigvec_rows, pltpu.HBM))
    halves = [list(range(half_devices)), list(range(half_devices, row_count))]
    lines = lax.all_to_all(lines, "row", 0, 0, axis_index_groups=halves)
    held = pl.pallas_call(
        functools.partial(held_kernel, height=height),
        out_shape=struct(lines_shape, eigvec_rows.dtype),
        in_specs=[smem, vmem],
        out_specs=vmem,
        compiler_params=limit(4),
        name="held_line",
    )(split, lines)
    flip = half_devices + half_devices // 2
    other = lax.ppermute(held, "row", [(i, i ^ flip) for i in range(row_count)])
    pole_lines = [pltpu.VMEM((1, width), jnp.float32)] * 2
    split_merged, part, sums = pl.pallas_call(
        functools.partial(merge_kernel, height=height, width=width, columns=width * col_count),
        out_shape=(
            struct((2 * panel, width), jnp.bfloat16),
            struct((panel, first), jnp.float32),
            struct((panel, LANES), jnp.float32),
        ),
        in_specs=[smem, vmem, vmem, vmem, vmem, vmem, vmem],
        out_specs=(vmem, vmem, vmem),
        scratch_shapes=[
            pltpu.VMEM((2 * width // LANES, LANES), jnp.float32),
            *pole_lines,
        ],
        compiler_params=limit(12),
        cost_estimate=pl.CostEstimate(flops=10**9, bytes_accessed=2**24, transcendentals=2**20),
        name="merge_columns",
    )(split, lines, eigvec_rows, shifts, deflate_mask, roots, panel_source)
    parts = pl.pallas_call(
        rest_kernel,
        out_shape=struct((col_count, panel // col_count, height + LANES), jnp.float32),
        in_specs=[vmem] * 8,
        out_specs=vmem,
        scratch_shapes=pole_lines,
        compiler_params=limit(12),
        cost_estimate=pl.CostEstimate(flops=10**9, bytes_accessed=2**23, transcendentals=2**20),
        name="rest_product",
    )(other, split_merged, eigvec_rows, part, sums, shifts, deflate_mask, roots)
    parts = lax.all_to_all(parts, "col", 0, 0)
    return pl.pallas_call(
        finish_kernel,
        out_shape=struct((panel // col_count, height), jnp.float32),
        in_specs=[vmem],
        out_specs=vmem,
        compiler_params=limit(4),
        name="scale_and_add",
    )(parts)


def solution(mesh):
    return jax.shard_map(
        local,
        mesh=mesh,
        in_specs=(P("row", "col"), P(), P(None, "col"), P(), P(None, "col"), P()),
        out_specs=P("col", "row"),
        check_vma=False,
    )
```

```python
import functools

import jax
import jax.numpy as jnp
from jax import lax
from jax.experimental import pallas as pl
from jax.experimental.pallas import tpu as pltpu
from jax.sharding import PartitionSpec as P

LANES = 128
ALIGN = 16
SUBLANES = 8
CHUNKS = 8


def pick_kernel(split_ref, rows_ref, out_ref, window, sem, *, height):
    half = lax.axis_index("row") // (lax.axis_size("row") // 2)
    row = split_ref[half] % height
    base = pl.multiple_of((row // ALIGN) * ALIGN, ALIGN)
    copy = pltpu.make_async_copy(rows_ref.at[pl.ds(base, ALIGN)], window, sem)
    copy.start()
    copy.wait()
    inner = row - base
    lower = inner < SUBLANES
    inner = lax.rem(inner, SUBLANES)
    sublane = lax.broadcasted_iota(jnp.int32, (SUBLANES, LANES), 0)
    blocks = [jnp.zeros((SUBLANES, LANES), jnp.float32) for _ in range(out_ref.shape[1] // SUBLANES)]
    for a in range(out_ref.shape[1]):
        both = window[:, a * LANES : (a + 1) * LANES].astype(jnp.float32)
        eight = jnp.where(lower, both[0:SUBLANES], both[SUBLANES:])
        target = a % SUBLANES
        turned = pltpu.roll(eight, lax.rem(target - inner + SUBLANES, SUBLANES), 0)
        blocks[a // SUBLANES] = jnp.where(sublane == target, turned, blocks[a // SUBLANES])
    line = jnp.concatenate(blocks, axis=0).astype(out_ref.dtype)
    for target in range(out_ref.shape[0]):
        out_ref[target] = line


def held_kernel(split_ref, lines_ref, out_ref, *, height):
    half = lax.axis_index("row") // (lax.axis_size("row") // 2)
    out_ref[...] = lines_ref[split_ref[half] // height]


def spread(line):
    return jnp.broadcast_to(line, (LANES, line.shape[1])).T


def merge_kernel(
    line_ref, _, shifts_ref, mask_ref, roots_ref, source_ref,
    split_out, sums_ref, kept_line, shift_line, *, columns
):
    half = lax.axis_index("row") // (lax.axis_size("row") // 2)
    col = lax.axis_index("col")
    panel = roots_ref.shape[1]
    tiles = line_ref.shape[0]
    width = tiles * LANES
    source = spread(source_ref[...])
    source_half = (source >= columns).astype(jnp.int32)
    local = source - source_half * columns - col * width
    here = (local >= 0) & (local < width)
    lane = lax.broadcasted_iota(jnp.int32, (panel, LANES), 1)
    tile_of = jnp.where(here, local // LANES * 2 + source_half, -1)
    picked = jnp.dot(
        jnp.where(lax.broadcasted_iota(jnp.int32, (panel, 2 * tiles), 1) == tile_of[:, 0:1], 1.0, 0.0).astype(jnp.bfloat16),
        mask_ref[...].astype(jnp.float32).astype(jnp.bfloat16),
        preferred_element_type=jnp.float32,
    )
    deflated = jnp.sum(jnp.where(lane == local % LANES, picked, 0.0), axis=1, keepdims=True) > 0.5
    own_flag = deflated & (source_half == half)
    roots_all = jnp.where(own_flag, 3e38, spread(roots_ref[...]))
    unit_all = jnp.where(own_flag, local, -1)
    first_lane = lax.broadcasted_iota(jnp.int32, (1, LANES), 1)
    kept_line[...] = jnp.where(mask_ref[pl.ds(half, tiles, stride=2), :] == 1, 0.0, line_ref[...].astype(jnp.float32))
    shift_line[...] = shifts_ref[pl.ds(half, tiles, stride=2), :]

    def fill(t, norm):
        at = pl.ds(pl.multiple_of(t * LANES, LANES), LANES)
        cauchy = kept_line[pl.ds(t, 1), :] * pltpu.reciprocal(shift_line[pl.ds(t, 1), :] - roots_all, approx=True)
        value = jnp.where(unit_all == first_lane + t * LANES, 1.0, cauchy)
        high = value.astype(jnp.bfloat16)
        split_out[0:panel, at] = high
        split_out[panel : 2 * panel, at] = (value - high.astype(jnp.float32)).astype(jnp.bfloat16)
        return norm + cauchy * cauchy

    norm = lax.fori_loop(0, tiles, fill, jnp.zeros((panel, LANES), jnp.float32), unroll=1)
    norm = jnp.sum(norm, axis=1, keepdims=True)
    own = jnp.where(own_flag, 1.0, 0.0)
    other = jnp.where(deflated & (source_half != half), 1.0, 0.0)
    sums_ref[...] = jnp.where(lane == 0, norm, jnp.where(lane == 1, own, jnp.where(lane == 2, other, 0.0)))


def product_kernel(
    other_ref, split_in, rows_ref, sums_ref, shifts_ref, mask_ref, roots_ref, out_ref, kept_line, shift_line
):
    other_half = 1 - lax.axis_index("row") // (lax.axis_size("row") // 2)
    panel = roots_ref.shape[1]
    groups, per_group, _ = out_ref.shape
    height, width = rows_ref.shape
    tiles = width // LANES
    kept_line[...] = jnp.where(
        mask_ref[pl.ds(other_half, tiles, stride=2), :] == 1, 0.0, other_ref[...].astype(jnp.float32)
    )
    shift_line[...] = shifts_ref[pl.ds(other_half, tiles, stride=2), :]
    roots_all = spread(roots_ref[...])
    norm = jnp.zeros((panel, LANES), jnp.float32)
    total = jnp.zeros((2 * panel, height), jnp.float32)
    chunk = width // CHUNKS
    for c in range(CHUNKS):
        at = slice(c * chunk, (c + 1) * chunk)
        total = total + lax.dot_general(
            split_in[:, at], rows_ref[:, at], (((1,), (1,)), ((), ())), preferred_element_type=jnp.float32
        )
        for t in range(c * chunk // LANES, (c + 1) * chunk // LANES):
            cauchy = kept_line[t : t + 1, :] * pltpu.reciprocal(shift_line[t : t + 1, :] - roots_all, approx=True)
            norm = norm + cauchy * cauchy
    lane = lax.broadcasted_iota(jnp.int32, (panel, LANES), 1)
    extra = sums_ref[...] + jnp.where(lane == 0, jnp.sum(norm, axis=1, keepdims=True), 0.0)
    out_ref[:, :, 0:height] = (total[0:panel] + total[panel : 2 * panel]).reshape(groups, per_group, height)
    out_ref[:, :, height:] = extra.reshape(groups, per_group, LANES)


def finish_kernel(parts_ref, out_ref):
    groups = parts_ref.shape[0]
    height = out_ref.shape[1]
    extra = parts_ref[:, :, height:]
    total = jnp.sum(extra, axis=0)
    norm2 = total[:, 0:1]
    deflated = total[:, 1:2] + total[:, 2:3] > 0.5
    scale = 1.0 / jnp.sqrt(norm2)
    result = jnp.zeros(out_ref.shape, jnp.float32)
    for group in range(groups):
        weight = jnp.where(deflated, extra[group, :, 1:2], scale)
        result = result + weight * parts_ref[group, :, 0:height]
    out_ref[...] = jnp.where(deflated & (total[:, 1:2] < 0.5), 0.0, result)


def local(eigvec_rows, split, shifts, roots, deflate_mask, panel_source):
    height, width = eigvec_rows.shape
    row_count = lax.axis_size("row")
    col_count = lax.axis_size("col")
    half_devices = row_count // 2
    panel = roots.shape[0]
    tiles = width // LANES
    vmem = pl.BlockSpec(memory_space=pltpu.VMEM)
    smem = pl.BlockSpec(memory_space=pltpu.SMEM)
    anywhere = pl.BlockSpec(memory_space=pl.ANY)
    limit = lambda mib: pltpu.CompilerParams(vmem_limit_bytes=mib * 2**20)
    in_hbm = lambda x: pltpu.with_memory_space_constraint(x, pltpu.HBM)
    square = lambda x: x.reshape(2, tiles, LANES).swapaxes(0, 1).reshape(2 * tiles, LANES)
    struct = jax.ShapeDtypeStruct
    roots = roots.reshape(1, -1)
    panel_source = panel_source.reshape(1, -1)
    shifts = square(shifts)
    deflate_mask = square(deflate_mask)
    lines = pl.pallas_call(
        functools.partial(pick_kernel, height=height),
        out_shape=struct((half_devices, tiles, LANES), eigvec_rows.dtype),
        in_specs=[smem, anywhere],
        out_specs=vmem,
        scratch_shapes=[pltpu.VMEM((ALIGN, width), eigvec_rows.dtype), pltpu.SemaphoreType.DMA],
        compiler_params=limit(4),
        name="pick_line",
    )(in_hbm(split), in_hbm(eigvec_rows))
    halves = [list(range(half_devices)), list(range(half_devices, row_count))]
    lines = lax.all_to_all(lines, "row", 0, 0, axis_index_groups=halves)
    line = pl.pallas_call(
        functools.partial(held_kernel, height=height),
        out_shape=struct((tiles, LANES), eigvec_rows.dtype),
        in_specs=[smem, vmem],
        out_specs=vmem,
        compiler_params=limit(4),
        name="held_line",
    )(split, lines)
    flip = half_devices + half_devices // 2
    other = lax.ppermute(line, "row", [(i, i ^ flip) for i in range(row_count)])
    pole_lines = [pltpu.VMEM((tiles, LANES), jnp.float32)] * 2
    split_merged, sums = pl.pallas_call(
        functools.partial(merge_kernel, columns=width * col_count),
        out_shape=(
            struct((2 * panel, width), jnp.bfloat16),
            struct((panel, LANES), jnp.float32),
        ),
        in_specs=[vmem] * 6,
        out_specs=(vmem, vmem),
        scratch_shapes=pole_lines,
        compiler_params=limit(8),
        cost_estimate=pl.CostEstimate(flops=10**9, bytes_accessed=2**24, transcendentals=2**20),
        name="merge_columns",
    )(line, eigvec_rows, shifts, deflate_mask, roots, panel_source)
    parts = pl.pallas_call(
        product_kernel,
        out_shape=struct((col_count, panel // col_count, height + LANES), jnp.float32),
        in_specs=[vmem] * 7,
        out_specs=vmem,
        scratch_shapes=pole_lines,
        compiler_params=limit(12),
        cost_estimate=pl.CostEstimate(flops=2 * 10**9, bytes_accessed=2**23, transcendentals=2**20),
        name="block_product",
    )(other, split_merged, eigvec_rows, sums, shifts, deflate_mask, roots)
    parts = lax.all_to_all(parts, "col", 0, 0)
    return pl.pallas_call(
        finish_kernel,
        out_shape=struct((panel // col_count, height), jnp.float32),
        in_specs=[vmem],
        out_specs=vmem,
        compiler_params=limit(4),
        name="scale_and_add",
    )(parts)


def solution(mesh):
    return jax.shard_map(
        local,
        mesh=mesh,
        in_specs=(P("row", "col"), P(), P(None, "col"), P(), P(None, "col"), P()),
        out_specs=P("col", "row"),
        check_vma=False,
    )
```

```python
import functools

import jax
import jax.numpy as jnp
from jax import lax
from jax.experimental import pallas as pl
from jax.experimental.pallas import tpu as pltpu
from jax.sharding import PartitionSpec as P

LANES = 128
ALIGN = 16
SUBLANES = 8
CHUNKS = 8


def pick_kernel(split_ref, rows_ref, out_ref, window, sem, *, height):
    half = lax.axis_index("row") // (lax.axis_size("row") // 2)
    row = split_ref[half] % height
    base = pl.multiple_of((row // ALIGN) * ALIGN, ALIGN)
    copy = pltpu.make_async_copy(rows_ref.at[pl.ds(base, ALIGN)], window, sem)
    copy.start()
    copy.wait()
    inner = row - base
    lower = inner < SUBLANES
    inner = lax.rem(inner, SUBLANES)
    sublane = lax.broadcasted_iota(jnp.int32, (SUBLANES, LANES), 0)
    blocks = [jnp.zeros((SUBLANES, LANES), jnp.float32) for _ in range(out_ref.shape[1] // SUBLANES)]
    for a in range(out_ref.shape[1]):
        both = window[:, a * LANES : (a + 1) * LANES].astype(jnp.float32)
        eight = jnp.where(lower, both[0:SUBLANES], both[SUBLANES:])
        target = a % SUBLANES
        turned = pltpu.roll(eight, lax.rem(target - inner + SUBLANES, SUBLANES), 0)
        blocks[a // SUBLANES] = jnp.where(sublane == target, turned, blocks[a // SUBLANES])
    line = jnp.concatenate(blocks, axis=0).astype(out_ref.dtype)
    for target in range(out_ref.shape[0]):
        out_ref[target] = line


def spread(line):
    return jnp.broadcast_to(line, (LANES, line.shape[1])).T


def norm_kernel(
    split_ref, lines_ref, _, shifts_ref, mask_ref, roots_ref, source_ref,
    norm_ref, sums_ref, kept_ref, own_shifts_ref, poles_ref, unit_ref, *, height, columns
):
    half = lax.axis_index("row") // (lax.axis_size("row") // 2)
    col = lax.axis_index("col")
    panel = roots_ref.shape[1]
    tiles = lines_ref.shape[1]
    width = tiles * LANES
    line = lines_ref[split_ref[half] // height].astype(jnp.float32)
    kept_ref[...] = jnp.where(mask_ref[pl.ds(half, tiles, stride=2), :] == 1, 0.0, line)
    own_shifts_ref[...] = shifts_ref[pl.ds(half, tiles, stride=2), :]
    roots_all = spread(roots_ref[...])
    source = spread(source_ref[...])
    source_half = (source >= columns).astype(jnp.int32)
    local = source - source_half * columns - col * width
    here = (local >= 0) & (local < width)
    lane = lax.broadcasted_iota(jnp.int32, (panel, LANES), 1)
    tile_of = jnp.where(here, local // LANES * 2 + source_half, -1)
    picked = jnp.dot(
        jnp.where(lax.broadcasted_iota(jnp.int32, (panel, 2 * tiles), 1) == tile_of[:, 0:1], 1.0, 0.0).astype(jnp.bfloat16),
        mask_ref[...].astype(jnp.float32).astype(jnp.bfloat16),
        preferred_element_type=jnp.float32,
    )
    deflated = jnp.sum(jnp.where(lane == local % LANES, picked, 0.0), axis=1, keepdims=True) > 0.5
    own_flag = deflated & (source_half == half)
    poles_ref[...] = jnp.where(own_flag, 3e38, roots_all)
    unit_ref[...] = jnp.where(own_flag, local, -1)
    norm = jnp.zeros((panel, LANES), jnp.float32)
    for t in range(tiles):
        cauchy = kept_ref[t : t + 1, :] * pltpu.reciprocal(own_shifts_ref[t : t + 1, :] - roots_all, approx=True)
        norm = norm + cauchy * cauchy
    norm = jnp.sum(norm, axis=1, keepdims=True)
    own = jnp.where(own_flag, 1.0, 0.0)
    other = jnp.where(deflated & (source_half != half), 1.0, 0.0)
    sums = jnp.where(lane == 0, norm, jnp.where(lane == 1, own, jnp.where(lane == 2, other, 0.0))).T[0:SUBLANES]
    norm_ref[...] = jnp.where(lax.broadcasted_iota(jnp.int32, (SUBLANES, LANES), 0) == 0, sums, 0.0)
    sums_ref[...] = sums


def product_kernel(kept_ref, shifts_ref, poles_ref, unit_ref, rows_ref, out_ref):
    panel = poles_ref.shape[0]
    groups = out_ref.shape[0]
    per_group = panel // groups
    height, width = rows_ref.shape
    poles = poles_ref[...]
    unit = unit_ref[...]
    lane = lax.broadcasted_iota(jnp.int32, (1, LANES), 1)
    total = jnp.zeros((2 * panel, height), jnp.float32)
    chunk = width // CHUNKS
    for c in range(CHUNKS):
        highs, lows = [], []
        for t in range(c * chunk // LANES, (c + 1) * chunk // LANES):
            cauchy = kept_ref[t : t + 1, :] * pltpu.reciprocal(shifts_ref[t : t + 1, :] - poles, approx=True)
            value = jnp.where(unit == lane + t * LANES, 1.0, cauchy)
            high = value.astype(jnp.bfloat16)
            highs.append(high)
            lows.append((value - high.astype(jnp.float32)).astype(jnp.bfloat16))
        merged = jnp.concatenate([jnp.concatenate(highs, axis=1), jnp.concatenate(lows, axis=1)], axis=0)
        total = total + lax.dot_general(
            merged, rows_ref[:, c * chunk : (c + 1) * chunk], (((1,), (1,)), ((), ())),
            preferred_element_type=jnp.float32,
        )
    product = (total[0:panel] + total[panel : 2 * panel]).reshape(groups, per_group, height)
    for q in range(height // LANES):
        out_ref[:, q * per_group : (q + 1) * per_group, :] = product[:, :, q * LANES : (q + 1) * LANES]
    out_ref[:, per_group * height // LANES :, :] = jnp.zeros((groups, SUBLANES, LANES), jnp.float32)


def finish_kernel(parts_ref, out_ref, columns_ref):
    groups = parts_ref.shape[0]
    per_group, height = out_ref.shape
    body = per_group * height // LANES
    columns_ref[...] = parts_ref[:, body:, :].reshape(groups * SUBLANES, LANES).T
    start = pl.multiple_of(lax.axis_index("col") * per_group, per_group)
    sums = columns_ref[pl.ds(start, per_group), :]
    kind = lax.broadcasted_iota(jnp.int32, sums.shape, 1) % SUBLANES
    norm2, own, other = (jnp.sum(jnp.where(kind == k, sums, 0.0), axis=1, keepdims=True) for k in range(3))
    scale = 1.0 / jnp.sqrt(norm2)
    blocks = [jnp.zeros((per_group, LANES), jnp.float32) for _ in range(height // LANES)]
    for group in range(groups):
        flag = sums[:, group * SUBLANES + 1 : group * SUBLANES + 2]
        weight = jnp.where(own + other > 0.5, flag, scale)
        for q in range(height // LANES):
            blocks[q] = blocks[q] + weight * parts_ref[group, q * per_group : (q + 1) * per_group, :]
    for q in range(height // LANES):
        out_ref[:, q * LANES : (q + 1) * LANES] = jnp.where(other > 0.5, 0.0, blocks[q])


def local(eigvec_rows, split, shifts, roots, deflate_mask, panel_source):
    height, width = eigvec_rows.shape
    row_count = lax.axis_size("row")
    col_count = lax.axis_size("col")
    half_devices = row_count // 2
    panel = roots.shape[0]
    tiles = width // LANES
    vmem = pl.BlockSpec(memory_space=pltpu.VMEM)
    smem = pl.BlockSpec(memory_space=pltpu.SMEM)
    anywhere = pl.BlockSpec(memory_space=pl.ANY)
    limit = lambda mib: pltpu.CompilerParams(vmem_limit_bytes=mib * 2**20)
    in_hbm = lambda x: pltpu.with_memory_space_constraint(x, pltpu.HBM)
    square = lambda x: x.reshape(2, tiles, LANES).swapaxes(0, 1).reshape(2 * tiles, LANES)
    struct = jax.ShapeDtypeStruct
    roots = roots.reshape(1, -1)
    panel_source = panel_source.reshape(1, -1)
    shifts = square(shifts)
    deflate_mask = square(deflate_mask)
    lines = pl.pallas_call(
        functools.partial(pick_kernel, height=height),
        out_shape=struct((half_devices, tiles, LANES), eigvec_rows.dtype),
        in_specs=[smem, anywhere],
        out_specs=vmem,
        scratch_shapes=[pltpu.VMEM((ALIGN, width), eigvec_rows.dtype), pltpu.SemaphoreType.DMA],
        compiler_params=limit(4),
        name="pick_line",
    )(in_hbm(split), in_hbm(eigvec_rows))
    halves = [list(range(half_devices)), list(range(half_devices, row_count))]
    lines = lax.all_to_all(lines, "row", 0, 0, axis_index_groups=halves)
    square_struct = struct((panel, LANES), jnp.float32)
    row_struct = struct((SUBLANES, panel), jnp.float32)
    line_struct = struct((tiles, LANES), jnp.float32)
    norm, sums, kept, own_shifts, poles, unit = pl.pallas_call(
        functools.partial(norm_kernel, height=height, columns=width * col_count),
        out_shape=(row_struct, row_struct, line_struct, line_struct, square_struct, struct((panel, LANES), jnp.int32)),
        in_specs=[smem] + [vmem] * 6,
        out_specs=(vmem,) * 6,
        compiler_params=limit(12),
        name="column_norms",
    )(split, lines, eigvec_rows, shifts, deflate_mask, roots, panel_source)
    flip = half_devices + half_devices // 2
    other = lax.ppermute(norm, "row", [(i, i ^ flip) for i in range(row_count)])
    body = panel // col_count * height // LANES
    parts = pl.pallas_call(
        product_kernel,
        out_shape=struct((col_count, body + SUBLANES, LANES), jnp.float32),
        in_specs=[vmem] * 5,
        out_specs=vmem,
        compiler_params=limit(16),
        cost_estimate=pl.CostEstimate(flops=2 * 10**9, bytes_accessed=2**24, transcendentals=2**20),
        name="block_product",
    )(kept, own_shifts, poles, unit, eigvec_rows)
    extra = jnp.broadcast_to(sums + other, (col_count, SUBLANES, LANES))
    parts = lax.dynamic_update_slice(parts, extra, (0, body, 0))
    parts = lax.all_to_all(parts, "col", 0, 0)
    return pl.pallas_call(
        finish_kernel,
        out_shape=struct((panel // col_count, height), jnp.float32),
        in_specs=[vmem],
        out_specs=vmem,
        scratch_shapes=[pltpu.VMEM((panel, col_count * SUBLANES), jnp.float32)],
        compiler_params=limit(4),
        name="scale_and_add",
    )(parts)


def solution(mesh):
    return jax.shard_map(
        local,
        mesh=mesh,
        in_specs=(P("row", "col"), P(), P(None, "col"), P(), P(None, "col"), P()),
        out_specs=P("col", "row"),
        check_vma=False,
    )
```

```python
import functools

import jax
import jax.numpy as jnp
from jax import lax
from jax.experimental import pallas as pl
from jax.experimental.pallas import tpu as pltpu
from jax.sharding import PartitionSpec as P

LANES = 128
ALIGN = 16
SUBLANES = 8
CHUNKS = 8
LOW_BLOCKS = 2


def spread(line):
    return jnp.broadcast_to(line, (LANES, line.shape[1])).T


def pick_kernel(
    split_hbm, rows_hbm, shifts_hbm, mask_hbm, roots_hbm, source_hbm,
    out_ref, own_mask_ref, own_shifts_ref, poles_ref, unit_ref, flags_ref, squares_ref,
    split_ref, window, shifts_ref, mask_ref, roots_ref, source_ref, sems, *, columns
):
    half = lax.axis_index("row") // (lax.axis_size("row") // 2)
    height, width = rows_hbm.shape
    panel = roots_ref.shape[1]
    tiles = width // LANES
    pairs = ((mask_hbm, mask_ref), (source_hbm, source_ref), (roots_hbm, roots_ref), (shifts_hbm, shifts_ref))
    split_copy = pltpu.make_async_copy(split_hbm, split_ref, sems.at[0])
    copies = [pltpu.make_async_copy(a, b, sems.at[i + 2]) for i, (a, b) in enumerate(pairs)]
    split_copy.start()
    for copy in copies:
        copy.start()
    split_copy.wait()
    row = split_ref[half] % height
    base = pl.multiple_of((row // ALIGN) * ALIGN, ALIGN)
    row_copy = pltpu.make_async_copy(rows_hbm.at[pl.ds(base, ALIGN)], window, sems.at[1])
    row_copy.start()
    for copy in copies:
        copy.wait()
    own_mask_ref[...] = mask_ref[pl.ds(half, tiles, stride=2), :]
    own_shifts_ref[...] = shifts_ref[pl.ds(half, tiles, stride=2), :]
    source = spread(source_ref[...])
    source_half = (source >= columns).astype(jnp.int32)
    local = source - source_half * columns - lax.axis_index("col") * width
    here = (local >= 0) & (local < width)
    lane = lax.broadcasted_iota(jnp.int32, (panel, LANES), 1)
    tile_of = jnp.where(here, local // LANES * 2 + source_half, -1)
    picked = jnp.dot(
        jnp.where(lax.broadcasted_iota(jnp.int32, (panel, 2 * tiles), 1) == tile_of[:, 0:1], 1.0, 0.0).astype(jnp.bfloat16),
        mask_ref[...].astype(jnp.float32).astype(jnp.bfloat16),
        preferred_element_type=jnp.float32,
    )
    deflated = jnp.sum(jnp.where(lane == local % LANES, picked, 0.0), axis=1, keepdims=True) > 0.5
    own_flag = deflated & (source_half == half)
    poles_ref[...] = jnp.where(own_flag, 3e38, spread(roots_ref[...]))
    unit_ref[...] = jnp.where(own_flag, local, -1)
    own = jnp.where(own_flag, 1.0, 0.0)
    other = jnp.where(deflated & (source_half != half), 1.0, 0.0)
    flags_ref[...] = jnp.where(lane == 1, own, jnp.where(lane == 2, other, 0.0)).T[0:SUBLANES]
    roots_all = spread(roots_ref[...])
    for t in range(tiles):
        inverse = pltpu.reciprocal(own_shifts_ref[t : t + 1, :] - roots_all, approx=True)
        squares_ref[:, t * LANES : (t + 1) * LANES] = inverse * inverse
    row_copy.wait()
    inner = row - base
    lower = inner < SUBLANES
    inner = lax.rem(inner, SUBLANES)
    sublane = lax.broadcasted_iota(jnp.int32, (SUBLANES, LANES), 0)
    blocks = [jnp.zeros((SUBLANES, LANES), jnp.float32) for _ in range(tiles // SUBLANES)]
    for t in range(tiles):
        both = window[:, t * LANES : (t + 1) * LANES].astype(jnp.float32)
        eight = jnp.where(lower, both[0:SUBLANES], both[SUBLANES:])
        target = t % SUBLANES
        turned = pltpu.roll(eight, lax.rem(target - inner + SUBLANES, SUBLANES), 0)
        blocks[t // SUBLANES] = jnp.where(sublane == target, turned, blocks[t // SUBLANES])
    line = jnp.concatenate(blocks, axis=0).astype(out_ref.dtype)
    for target in range(out_ref.shape[0]):
        out_ref[target] = line


def norm_kernel(
    split_ref, lines_ref, mask_ref, squares_ref, flags_ref, norm_ref, sums_ref, kept_ref, line_ref, *, height
):
    half = lax.axis_index("row") // (lax.axis_size("row") // 2)
    panel = squares_ref.shape[0]
    tiles = lines_ref.shape[1]
    line = lines_ref[split_ref[half] // height].astype(jnp.float32)
    kept = jnp.where(mask_ref[...] == 1, 0.0, line)
    kept_ref[...] = kept
    line_ref[...] = kept * kept
    norm = jnp.zeros((panel, LANES), jnp.float32)
    for t in range(tiles):
        norm = norm + line_ref[t : t + 1, :] * squares_ref[:, t * LANES : (t + 1) * LANES]
    lane = lax.broadcasted_iota(jnp.int32, (panel, LANES), 1)
    norm = jnp.where(lane == 0, jnp.sum(norm, axis=1, keepdims=True), 0.0).T[0:SUBLANES]
    norm_ref[...] = norm
    sums_ref[...] = norm + flags_ref[...]


def product_kernel(kept_ref, shifts_ref, poles_ref, unit_ref, rows_ref, out_ref):
    panel = poles_ref.shape[0]
    groups = out_ref.shape[0]
    per_group = panel // groups
    height, width = rows_ref.shape
    poles = poles_ref[...]
    unit = unit_ref[...]
    lane = lax.broadcasted_iota(jnp.int32, (1, LANES), 1)
    total = jnp.zeros((2 * panel, height), jnp.float32)
    chunk = width // CHUNKS
    for c in range(CHUNKS):
        highs, lows = [], []
        for t in range(c * chunk // LANES, (c + 1) * chunk // LANES):
            cauchy = kept_ref[t : t + 1, :] * pltpu.reciprocal(shifts_ref[t : t + 1, :] - poles, approx=True)
            value = jnp.where(unit == lane + t * LANES, 1.0, cauchy)
            high = value.astype(jnp.bfloat16)
            highs.append(high)
            lows.append((value - high.astype(jnp.float32)).astype(jnp.bfloat16))
        merged = jnp.concatenate([jnp.concatenate(highs, axis=1), jnp.concatenate(lows, axis=1)], axis=0)
        total = total + lax.dot_general(
            merged, rows_ref[:, c * chunk : (c + 1) * chunk], (((1,), (1,)), ((), ())),
            preferred_element_type=jnp.float32,
        )
    product = (total[0:panel] + total[panel : 2 * panel]).reshape(groups, per_group, height)
    blocks = height // LANES
    for q in range(blocks):
        block = product[:, :, q * LANES : (q + 1) * LANES]
        high = block.astype(jnp.bfloat16)
        out_ref[:, q * per_group : (q + 1) * per_group, :] = high
        if q < LOW_BLOCKS:
            low = (block - high.astype(jnp.float32)).astype(jnp.bfloat16)
            out_ref[:, (blocks + q) * per_group : (blocks + q + 1) * per_group, :] = low
    extra = (blocks + LOW_BLOCKS) * per_group
    out_ref[:, extra:, :] = jnp.zeros((groups, ALIGN, LANES), jnp.bfloat16)


def finish_kernel(parts_ref, out_ref, columns_ref):
    groups = parts_ref.shape[0]
    per_group, height = out_ref.shape
    blocks = height // LANES
    extra = (blocks + LOW_BLOCKS) * per_group
    columns_ref[...] = parts_ref[:, extra:, :].astype(jnp.float32).reshape(groups * ALIGN, LANES).T
    start = pl.multiple_of(lax.axis_index("col") * per_group, per_group)
    sums = columns_ref[pl.ds(start, per_group), :]
    kind = lax.broadcasted_iota(jnp.int32, sums.shape, 1) % ALIGN
    total = lambda chosen: jnp.sum(jnp.where(chosen, sums, 0.0), axis=1, keepdims=True)
    norm2, own, other = total((kind == 0) | (kind == SUBLANES)), total(kind == 1), total(kind == 2)
    scale = 1.0 / jnp.sqrt(norm2)
    results = [jnp.zeros((per_group, LANES), jnp.float32) for _ in range(blocks)]
    for group in range(groups):
        flag = sums[:, group * ALIGN + 1 : group * ALIGN + 2]
        weight = jnp.where(own + other > 0.5, flag, scale)
        for q in range(blocks):
            value = parts_ref[group, q * per_group : (q + 1) * per_group, :].astype(jnp.float32)
            if q < LOW_BLOCKS:
                low = parts_ref[group, (blocks + q) * per_group : (blocks + q + 1) * per_group, :]
                value = value + low.astype(jnp.float32)
            results[q] = results[q] + weight * value
    for q in range(blocks):
        out_ref[:, q * LANES : (q + 1) * LANES] = jnp.where(other > 0.5, 0.0, results[q])


def local(eigvec_rows, split, shifts, roots, deflate_mask, panel_source):
    height, width = eigvec_rows.shape
    row_count = lax.axis_size("row")
    col_count = lax.axis_size("col")
    half_devices = row_count // 2
    panel = roots.shape[0]
    tiles = width // LANES
    vmem = pl.BlockSpec(memory_space=pltpu.VMEM)
    smem = pl.BlockSpec(memory_space=pltpu.SMEM)
    anywhere = pl.BlockSpec(memory_space=pl.ANY)
    limit = lambda mib: pltpu.CompilerParams(vmem_limit_bytes=mib * 2**20)
    in_hbm = lambda x: pltpu.with_memory_space_constraint(x, pltpu.HBM)
    square = lambda x: x.reshape(2, tiles, LANES).swapaxes(0, 1).reshape(2 * tiles, LANES)
    struct = jax.ShapeDtypeStruct
    roots = roots.reshape(1, -1)
    panel_source = panel_source.reshape(1, -1)
    shifts = square(shifts)
    deflate_mask = square(deflate_mask)
    row_struct = struct((SUBLANES, panel), jnp.float32)
    line_struct = lambda kind: struct((tiles, LANES), kind)
    square_struct = lambda kind: struct((panel, LANES), kind)
    lines, own_mask, own_shifts, poles, unit, flags, squares = pl.pallas_call(
        functools.partial(pick_kernel, columns=width * col_count),
        out_shape=(
            struct((half_devices, tiles, LANES), eigvec_rows.dtype),
            line_struct(jnp.int32),
            line_struct(jnp.float32),
            square_struct(jnp.float32),
            square_struct(jnp.int32),
            row_struct,
            struct((panel, width), jnp.float32),
        ),
        in_specs=[anywhere] * 6,
        out_specs=(vmem,) * 7,
        scratch_shapes=[
            pltpu.SMEM((2,), jnp.int32),
            pltpu.VMEM((ALIGN, width), eigvec_rows.dtype),
            pltpu.VMEM((2 * tiles, LANES), jnp.float32),
            pltpu.VMEM((2 * tiles, LANES), jnp.int32),
            pltpu.VMEM((1, panel), jnp.float32),
            pltpu.VMEM((1, panel), jnp.int32),
            pltpu.SemaphoreType.DMA((6,)),
        ],
        compiler_params=limit(4),
        name="pick_line",
    )(*[in_hbm(x) for x in (split, eigvec_rows, shifts, deflate_mask, roots, panel_source)])
    halves = [list(range(half_devices)), list(range(half_devices, row_count))]
    lines = lax.all_to_all(lines, "row", 0, 0, axis_index_groups=halves)
    norm, sums, kept = pl.pallas_call(
        functools.partial(norm_kernel, height=height),
        out_shape=(row_struct, row_struct, line_struct(jnp.float32)),
        in_specs=[smem] + [vmem] * 4,
        out_specs=(vmem,) * 3,
        scratch_shapes=[pltpu.VMEM((tiles, LANES), jnp.float32)],
        compiler_params=limit(8),
        name="column_norms",
    )(split, lines, own_mask, squares, flags)
    flip = half_devices + half_devices // 2
    other = lax.ppermute(norm, "row", [(i, i ^ flip) for i in range(row_count)])
    body = panel // col_count * (height // LANES + LOW_BLOCKS)
    parts = pl.pallas_call(
        product_kernel,
        out_shape=struct((col_count, body + ALIGN, LANES), jnp.bfloat16),
        in_specs=[vmem] * 5,
        out_specs=vmem,
        compiler_params=limit(16),
        cost_estimate=pl.CostEstimate(flops=2 * 10**9, bytes_accessed=2**24, transcendentals=2**20),
        name="block_product",
    )(kept, own_shifts, poles, unit, eigvec_rows)
    norms = sums + other
    first = lax.reduce_precision(norms, 8, 7)
    extra = jnp.concatenate([first, norms - first]).astype(jnp.bfloat16)
    extra = jnp.broadcast_to(extra, (col_count, ALIGN, LANES))
    parts = lax.dynamic_update_slice(parts, extra, (0, body, 0))
    parts = lax.all_to_all(parts, "col", 0, 0)
    return pl.pallas_call(
        finish_kernel,
        out_shape=struct((panel // col_count, height), jnp.float32),
        in_specs=[vmem],
        out_specs=vmem,
        scratch_shapes=[pltpu.VMEM((panel, col_count * ALIGN), jnp.float32)],
        compiler_params=limit(4),
        name="scale_and_add",
    )(parts)


def solution(mesh):
    return jax.shard_map(
        local,
        mesh=mesh,
        in_specs=(P("row", "col"), P(), P(None, "col"), P(), P(None, "col"), P()),
        out_specs=P("col", "row"),
        check_vma=False,
    )
```

```python
import functools

import jax
import jax.numpy as jnp
from jax import lax
from jax.experimental import pallas as pl
from jax.experimental.pallas import tpu as pltpu
from jax.sharding import PartitionSpec as P

LANES = 128
ALIGN = 16
SUBLANES = 8
CHUNKS = 8
LOW_BLOCKS = 2


def spread(line):
    return jnp.broadcast_to(line, (LANES, line.shape[1])).T


def pick_kernel(
    split_hbm, rows_hbm, shifts_hbm, mask_hbm, roots_hbm, source_hbm,
    out_ref, own_mask_ref, own_shifts_ref, poles_ref, unit_ref, flags_ref, squares_ref, holder_ref,
    split_ref, window, shifts_ref, mask_ref, roots_ref, source_ref, sems, *, columns
):
    half = lax.axis_index("row") // (lax.axis_size("row") // 2)
    height, width = rows_hbm.shape
    panel = roots_ref.shape[1]
    tiles = width // LANES
    pairs = ((mask_hbm, mask_ref), (source_hbm, source_ref), (roots_hbm, roots_ref), (shifts_hbm, shifts_ref))
    split_copy = pltpu.make_async_copy(split_hbm, split_ref, sems.at[0])
    copies = [pltpu.make_async_copy(a, b, sems.at[i + 2]) for i, (a, b) in enumerate(pairs)]
    split_copy.start()
    for copy in copies:
        copy.start()
    split_copy.wait()
    row = split_ref[half] % height
    device = lax.broadcasted_iota(jnp.int32, holder_ref.shape, 0)
    holder_ref[...] = jnp.where(device == split_ref[half] // height, 1.0, 0.0)
    base = pl.multiple_of((row // ALIGN) * ALIGN, ALIGN)
    row_copy = pltpu.make_async_copy(rows_hbm.at[pl.ds(base, ALIGN)], window, sems.at[1])
    row_copy.start()
    for copy in copies:
        copy.wait()
    own_mask_ref[...] = mask_ref[pl.ds(half, tiles, stride=2), :]
    own_shifts_ref[...] = shifts_ref[pl.ds(half, tiles, stride=2), :]
    source = spread(source_ref[...])
    source_half = (source >= columns).astype(jnp.int32)
    local = source - source_half * columns - lax.axis_index("col") * width
    here = (local >= 0) & (local < width)
    lane = lax.broadcasted_iota(jnp.int32, (panel, LANES), 1)
    tile_of = jnp.where(here, local // LANES * 2 + source_half, -1)
    picked = jnp.dot(
        jnp.where(lax.broadcasted_iota(jnp.int32, (panel, 2 * tiles), 1) == tile_of[:, 0:1], 1.0, 0.0).astype(jnp.bfloat16),
        mask_ref[...].astype(jnp.float32).astype(jnp.bfloat16),
        preferred_element_type=jnp.float32,
    )
    deflated = jnp.sum(jnp.where(lane == local % LANES, picked, 0.0), axis=1, keepdims=True) > 0.5
    own_flag = deflated & (source_half == half)
    poles_ref[...] = jnp.where(own_flag, 3e38, spread(roots_ref[...]))
    unit_ref[...] = jnp.where(own_flag, local, -1)
    own = jnp.where(own_flag, 1.0, 0.0)
    other = jnp.where(deflated & (source_half != half), 1.0, 0.0)
    flags_ref[...] = jnp.where(lane == 1, own, jnp.where(lane == 2, other, 0.0)).T[0:SUBLANES]
    roots_all = spread(roots_ref[...])
    for t in range(tiles):
        inverse = pltpu.reciprocal(own_shifts_ref[t : t + 1, :] - roots_all, approx=True)
        squares_ref[:, t * LANES : (t + 1) * LANES] = inverse * inverse
    row_copy.wait()
    inner = row - base
    lower = inner < SUBLANES
    inner = lax.rem(inner, SUBLANES)
    sublane = lax.broadcasted_iota(jnp.int32, (SUBLANES, LANES), 0)
    blocks = [jnp.zeros((SUBLANES, LANES), jnp.float32) for _ in range(tiles // SUBLANES)]
    for t in range(tiles):
        both = window[:, t * LANES : (t + 1) * LANES].astype(jnp.float32)
        eight = jnp.where(lower, both[0:SUBLANES], both[SUBLANES:])
        target = t % SUBLANES
        turned = pltpu.roll(eight, lax.rem(target - inner + SUBLANES, SUBLANES), 0)
        blocks[t // SUBLANES] = jnp.where(sublane == target, turned, blocks[t // SUBLANES])
    line = jnp.concatenate(blocks, axis=0).astype(out_ref.dtype)
    for target in range(out_ref.shape[0]):
        out_ref[target] = line


def norm_kernel(
    holder_ref, lines_ref, mask_ref, squares_ref, flags_ref, norm_ref, sums_ref, kept_ref, line_ref
):
    panel = squares_ref.shape[0]
    tiles = lines_ref.shape[1]
    line = jnp.zeros((tiles, LANES), jnp.float32)
    for device in range(lines_ref.shape[0]):
        line = jnp.where(holder_ref[device : device + 1, :] > 0.5, lines_ref[device].astype(jnp.float32), line)
    kept = jnp.where(mask_ref[...] == 1, 0.0, line)
    kept_ref[...] = kept
    line_ref[...] = kept * kept
    norm = jnp.zeros((panel, LANES), jnp.float32)
    for t in range(tiles):
        norm = norm + line_ref[t : t + 1, :] * squares_ref[:, t * LANES : (t + 1) * LANES]
    lane = lax.broadcasted_iota(jnp.int32, (panel, LANES), 1)
    norm = jnp.where(lane == 0, jnp.sum(norm, axis=1, keepdims=True), 0.0).T[0:SUBLANES]
    norm_ref[...] = norm
    sums_ref[...] = norm + flags_ref[...]


def product_kernel(kept_ref, shifts_ref, poles_ref, unit_ref, rows_ref, out_ref):
    panel = poles_ref.shape[0]
    groups = out_ref.shape[0]
    per_group = panel // groups
    height, width = rows_ref.shape
    poles = poles_ref[...]
    unit = unit_ref[...]
    lane = lax.broadcasted_iota(jnp.int32, (1, LANES), 1)
    total = jnp.zeros((2 * panel, height), jnp.float32)
    chunk = width // CHUNKS
    for c in range(CHUNKS):
        highs, lows = [], []
        for t in range(c * chunk // LANES, (c + 1) * chunk // LANES):
            cauchy = kept_ref[t : t + 1, :] * pltpu.reciprocal(shifts_ref[t : t + 1, :] - poles, approx=True)
            value = jnp.where(unit == lane + t * LANES, 1.0, cauchy)
            high = value.astype(jnp.bfloat16)
            highs.append(high)
            lows.append((value - high.astype(jnp.float32)).astype(jnp.bfloat16))
        merged = jnp.concatenate([jnp.concatenate(highs, axis=1), jnp.concatenate(lows, axis=1)], axis=0)
        total = total + lax.dot_general(
            merged, rows_ref[:, c * chunk : (c + 1) * chunk], (((1,), (1,)), ((), ())),
            preferred_element_type=jnp.float32,
        )
    product = (total[0:panel] + total[panel : 2 * panel]).reshape(groups, per_group, height)
    blocks = height // LANES
    for q in range(blocks):
        block = product[:, :, q * LANES : (q + 1) * LANES]
        high = block.astype(jnp.bfloat16)
        out_ref[:, q * per_group : (q + 1) * per_group, :] = high
        if q < LOW_BLOCKS:
            low = (block - high.astype(jnp.float32)).astype(jnp.bfloat16)
            out_ref[:, (blocks + q) * per_group : (blocks + q + 1) * per_group, :] = low
    extra = (blocks + LOW_BLOCKS) * per_group
    out_ref[:, extra:, :] = jnp.zeros((groups, ALIGN, LANES), jnp.bfloat16)


def finish_kernel(parts_ref, out_ref, columns_ref):
    groups = parts_ref.shape[0]
    per_group, height = out_ref.shape
    blocks = height // LANES
    extra = (blocks + LOW_BLOCKS) * per_group
    columns_ref[...] = parts_ref[:, extra:, :].astype(jnp.float32).reshape(groups * ALIGN, LANES).T
    start = pl.multiple_of(lax.axis_index("col") * per_group, per_group)
    sums = columns_ref[pl.ds(start, per_group), :]
    kind = lax.broadcasted_iota(jnp.int32, sums.shape, 1) % ALIGN
    total = lambda chosen: jnp.sum(jnp.where(chosen, sums, 0.0), axis=1, keepdims=True)
    norm2, own, other = total((kind == 0) | (kind == SUBLANES)), total(kind == 1), total(kind == 2)
    scale = 1.0 / jnp.sqrt(norm2)
    results = [jnp.zeros((per_group, LANES), jnp.float32) for _ in range(blocks)]
    for group in range(groups):
        flag = sums[:, group * ALIGN + 1 : group * ALIGN + 2]
        weight = jnp.where(own + other > 0.5, flag, scale)
        for q in range(blocks):
            value = parts_ref[group, q * per_group : (q + 1) * per_group, :].astype(jnp.float32)
            if q < LOW_BLOCKS:
                low = parts_ref[group, (blocks + q) * per_group : (blocks + q + 1) * per_group, :]
                value = value + low.astype(jnp.float32)
            results[q] = results[q] + weight * value
    for q in range(blocks):
        out_ref[:, q * LANES : (q + 1) * LANES] = jnp.where(other > 0.5, 0.0, results[q])


def local(eigvec_rows, split, shifts, roots, deflate_mask, panel_source):
    height, width = eigvec_rows.shape
    row_count = lax.axis_size("row")
    col_count = lax.axis_size("col")
    half_devices = row_count // 2
    panel = roots.shape[0]
    tiles = width // LANES
    vmem = pl.BlockSpec(memory_space=pltpu.VMEM)
    anywhere = pl.BlockSpec(memory_space=pl.ANY)
    limit = lambda mib: pltpu.CompilerParams(vmem_limit_bytes=mib * 2**20)
    in_hbm = lambda x: pltpu.with_memory_space_constraint(x, pltpu.HBM)
    square = lambda x: x.reshape(2, tiles, LANES).swapaxes(0, 1).reshape(2 * tiles, LANES)
    struct = jax.ShapeDtypeStruct
    roots = roots.reshape(1, -1)
    panel_source = panel_source.reshape(1, -1)
    shifts = square(shifts)
    deflate_mask = square(deflate_mask)
    row_struct = struct((SUBLANES, panel), jnp.float32)
    line_struct = lambda kind: struct((tiles, LANES), kind)
    square_struct = lambda kind: struct((panel, LANES), kind)
    lines, own_mask, own_shifts, poles, unit, flags, squares, holder = pl.pallas_call(
        functools.partial(pick_kernel, columns=width * col_count),
        out_shape=(
            struct((half_devices, tiles, LANES), eigvec_rows.dtype),
            line_struct(jnp.int32),
            line_struct(jnp.float32),
            square_struct(jnp.float32),
            square_struct(jnp.int32),
            row_struct,
            struct((panel, width), jnp.float32),
            struct((half_devices, LANES), jnp.float32),
        ),
        in_specs=[anywhere] * 6,
        out_specs=(vmem,) * 8,
        scratch_shapes=[
            pltpu.SMEM((2,), jnp.int32),
            pltpu.VMEM((ALIGN, width), eigvec_rows.dtype),
            pltpu.VMEM((2 * tiles, LANES), jnp.float32),
            pltpu.VMEM((2 * tiles, LANES), jnp.int32),
            pltpu.VMEM((1, panel), jnp.float32),
            pltpu.VMEM((1, panel), jnp.int32),
            pltpu.SemaphoreType.DMA((6,)),
        ],
        compiler_params=limit(4),
        name="pick_line",
    )(*[in_hbm(x) for x in (split, eigvec_rows, shifts, deflate_mask, roots, panel_source)])
    halves = [list(range(half_devices)), list(range(half_devices, row_count))]
    lines = lax.all_to_all(lines, "row", 0, 0, axis_index_groups=halves)
    norm, sums, kept = pl.pallas_call(
        norm_kernel,
        out_shape=(row_struct, row_struct, line_struct(jnp.float32)),
        in_specs=[vmem] * 5,
        out_specs=(vmem,) * 3,
        scratch_shapes=[pltpu.VMEM((tiles, LANES), jnp.float32)],
        compiler_params=limit(8),
        name="column_norms",
    )(holder, lines, own_mask, squares, flags)
    flip = half_devices + half_devices // 2
    other = lax.ppermute(norm, "row", [(i, i ^ flip) for i in range(row_count)])
    body = panel // col_count * (height // LANES + LOW_BLOCKS)
    parts = pl.pallas_call(
        product_kernel,
        out_shape=struct((col_count, body + ALIGN, LANES), jnp.bfloat16),
        in_specs=[vmem] * 5,
        out_specs=vmem,
        compiler_params=limit(16),
        cost_estimate=pl.CostEstimate(flops=2 * 10**9, bytes_accessed=2**24, transcendentals=2**20),
        name="block_product",
    )(kept, own_shifts, poles, unit, eigvec_rows)
    norms = sums + other
    first = lax.reduce_precision(norms, 8, 7)
    extra = jnp.concatenate([first, norms - first]).astype(jnp.bfloat16)
    extra = jnp.broadcast_to(extra, (col_count, ALIGN, LANES))
    parts = lax.dynamic_update_slice(parts, extra, (0, body, 0))
    parts = lax.all_to_all(parts, "col", 0, 0)
    return pl.pallas_call(
        finish_kernel,
        out_shape=struct((panel // col_count, height), jnp.float32),
        in_specs=[vmem],
        out_specs=vmem,
        scratch_shapes=[pltpu.VMEM((panel, col_count * ALIGN), jnp.float32)],
        compiler_params=limit(4),
        name="scale_and_add",
    )(parts)


def solution(mesh):
    return jax.shard_map(
        local,
        mesh=mesh,
        in_specs=(P("row", "col"), P(), P(None, "col"), P(), P(None, "col"), P()),
        out_specs=P("col", "row"),
        check_vma=False,
    )
```

```python
import functools

import jax
import jax.numpy as jnp
from jax import lax
from jax.experimental import pallas as pl
from jax.experimental.pallas import tpu as pltpu
from jax.sharding import PartitionSpec as P

LANES = 128
ALIGN = 16
SUBLANES = 8
CHUNKS = 8
LOW_BLOCKS = 2


def spread(line):
    return jnp.broadcast_to(line, (LANES, line.shape[1])).T


def pick_kernel(
    split_hbm, rows_hbm, shifts_hbm, mask_hbm, roots_hbm, source_hbm,
    out_ref, own_mask_ref, own_shifts_ref, poles_ref, unit_ref, flags_ref, squares_ref, holder_ref,
    split_ref, window, shifts_ref, mask_ref, roots_ref, source_ref, sems, *, columns
):
    half = lax.axis_index("row") // (lax.axis_size("row") // 2)
    height, width = rows_hbm.shape
    panel = roots_ref.shape[1]
    tiles = width // LANES
    pairs = ((mask_hbm, mask_ref), (source_hbm, source_ref), (roots_hbm, roots_ref), (shifts_hbm, shifts_ref))
    split_copy = pltpu.make_async_copy(split_hbm, split_ref, sems.at[0])
    copies = [pltpu.make_async_copy(a, b, sems.at[i + 2]) for i, (a, b) in enumerate(pairs)]
    split_copy.start()
    for copy in copies:
        copy.start()
    split_copy.wait()
    row = split_ref[half] % height
    device = lax.broadcasted_iota(jnp.int32, holder_ref.shape, 0)
    holder_ref[...] = jnp.where(device == split_ref[half] // height, 1.0, 0.0)
    base = pl.multiple_of((row // ALIGN) * ALIGN, ALIGN)
    row_copy = pltpu.make_async_copy(rows_hbm.at[pl.ds(base, ALIGN)], window, sems.at[1])
    row_copy.start()
    for copy in copies:
        copy.wait()
    own_mask_ref[...] = mask_ref[pl.ds(half, tiles, stride=2), :]
    own_shifts_ref[...] = shifts_ref[pl.ds(half, tiles, stride=2), :]
    source = spread(source_ref[...])
    source_half = (source >= columns).astype(jnp.int32)
    local = source - source_half * columns - lax.axis_index("col") * width
    here = (local >= 0) & (local < width)
    lane = lax.broadcasted_iota(jnp.int32, (panel, LANES), 1)
    tile_of = jnp.where(here, local // LANES * 2 + source_half, -1)
    picked = jnp.dot(
        jnp.where(lax.broadcasted_iota(jnp.int32, (panel, 2 * tiles), 1) == tile_of[:, 0:1], 1.0, 0.0).astype(jnp.bfloat16),
        mask_ref[...].astype(jnp.float32).astype(jnp.bfloat16),
        preferred_element_type=jnp.float32,
    )
    deflated = jnp.sum(jnp.where(lane == local % LANES, picked, 0.0), axis=1, keepdims=True) > 0.5
    own_flag = deflated & (source_half == half)
    poles_ref[...] = jnp.where(own_flag, 3e38, spread(roots_ref[...]))
    unit_ref[...] = jnp.where(own_flag, local, -1)
    own = jnp.where(own_flag, 1.0, 0.0)
    other = jnp.where(deflated & (source_half != half), 1.0, 0.0)
    flags_ref[...] = jnp.where(lane == 1, own, jnp.where(lane == 2, other, 0.0)).T[0:SUBLANES]
    roots_all = spread(roots_ref[...])
    for t in range(tiles):
        inverse = pltpu.reciprocal(own_shifts_ref[t : t + 1, :] - roots_all, approx=True)
        squares_ref[:, t * LANES : (t + 1) * LANES] = inverse * inverse
    row_copy.wait()
    inner = row - base
    lower = inner < SUBLANES
    inner = lax.rem(inner, SUBLANES)
    sublane = lax.broadcasted_iota(jnp.int32, (SUBLANES, LANES), 0)
    blocks = [jnp.zeros((SUBLANES, LANES), jnp.float32) for _ in range(tiles // SUBLANES)]
    for t in range(tiles):
        both = window[:, t * LANES : (t + 1) * LANES].astype(jnp.float32)
        eight = jnp.where(lower, both[0:SUBLANES], both[SUBLANES:])
        target = t % SUBLANES
        turned = pltpu.roll(eight, lax.rem(target - inner + SUBLANES, SUBLANES), 0)
        blocks[t // SUBLANES] = jnp.where(sublane == target, turned, blocks[t // SUBLANES])
    line = jnp.concatenate(blocks, axis=0).astype(out_ref.dtype)
    for target in range(out_ref.shape[0]):
        out_ref[target] = line


def norm_kernel(
    holder_ref, lines_ref, mask_ref, squares_ref, flags_ref, norm_ref, sums_ref, kept_ref, line_ref
):
    panel = squares_ref.shape[0]
    tiles = lines_ref.shape[1]
    line = jnp.zeros((tiles, LANES), jnp.float32)
    for device in range(lines_ref.shape[0]):
        line = jnp.where(holder_ref[device : device + 1, :] > 0.5, lines_ref[device].astype(jnp.float32), line)
    kept = jnp.where(mask_ref[...] == 1, 0.0, line)
    kept_ref[...] = kept
    line_ref[...] = kept * kept
    norm = jnp.zeros((panel, LANES), jnp.float32)
    for t in range(tiles):
        norm = norm + line_ref[t : t + 1, :] * squares_ref[:, t * LANES : (t + 1) * LANES]
    lane = lax.broadcasted_iota(jnp.int32, (panel, LANES), 1)
    norm = jnp.where(lane == 0, jnp.sum(norm, axis=1, keepdims=True), 0.0).T[0:SUBLANES]
    norm_ref[...] = norm
    sums_ref[...] = norm + flags_ref[...]


def product_kernel(kept_ref, shifts_ref, poles_ref, unit_ref, rows_ref, out_ref):
    panel = poles_ref.shape[0]
    groups = out_ref.shape[0]
    per_group = panel // groups
    height, width = rows_ref.shape
    poles = poles_ref[...]
    unit = unit_ref[...]
    lane = lax.broadcasted_iota(jnp.int32, (1, LANES), 1)
    total = jnp.zeros((2 * panel, height), jnp.float32)
    chunk = width // CHUNKS
    for c in range(CHUNKS):
        highs, lows = [], []
        for t in range(c * chunk // LANES, (c + 1) * chunk // LANES):
            cauchy = kept_ref[t : t + 1, :] * pltpu.reciprocal(shifts_ref[t : t + 1, :] - poles, approx=True)
            value = jnp.where(unit == lane + t * LANES, 1.0, cauchy)
            high = value.astype(jnp.bfloat16)
            highs.append(high)
            lows.append((value - high.astype(jnp.float32)).astype(jnp.bfloat16))
        merged = jnp.concatenate([jnp.concatenate(highs, axis=1), jnp.concatenate(lows, axis=1)], axis=0)
        total = total + lax.dot_general(
            merged, rows_ref[:, c * chunk : (c + 1) * chunk], (((1,), (1,)), ((), ())),
            preferred_element_type=jnp.float32,
        )
    product = (total[0:panel] + total[panel : 2 * panel]).reshape(groups, per_group, height)
    blocks = height // LANES
    for q in range(blocks):
        block = product[:, :, q * LANES : (q + 1) * LANES]
        high = block.astype(jnp.bfloat16)
        out_ref[:, q * per_group : (q + 1) * per_group, :] = high
        if q < LOW_BLOCKS:
            low = (block - high.astype(jnp.float32)).astype(jnp.bfloat16)
            out_ref[:, (blocks + q) * per_group : (blocks + q + 1) * per_group, :] = low
    extra = (blocks + LOW_BLOCKS) * per_group
    out_ref[:, extra:, :] = jnp.zeros((groups, ALIGN, LANES), jnp.bfloat16)


def finish_kernel(parts_ref, out_ref, columns_ref):
    groups = parts_ref.shape[0]
    per_group, height = out_ref.shape
    blocks = height // LANES
    extra = (blocks + LOW_BLOCKS) * per_group
    rows = parts_ref[:, extra:, :].astype(jnp.float32)
    total = jnp.sum(rows, axis=0)
    norm2, own, other = total[0:1] + total[SUBLANES : SUBLANES + 1], total[1:2], total[2:3]
    scale = jnp.where(other > 0.5, 0.0, 1.0 / jnp.sqrt(norm2))
    weights = [jnp.where(own > 0.5, rows[group, 1:2], scale) for group in range(groups)]
    columns_ref[...] = jnp.concatenate(weights, axis=0).T
    start = pl.multiple_of(lax.axis_index("col") * per_group, per_group)
    weights = columns_ref[pl.ds(start, per_group), :]
    results = [jnp.zeros((per_group, LANES), jnp.float32) for _ in range(blocks)]
    for group in range(groups):
        weight = weights[:, group : group + 1]
        for q in range(blocks):
            value = parts_ref[group, q * per_group : (q + 1) * per_group, :].astype(jnp.float32)
            if q < LOW_BLOCKS:
                low = parts_ref[group, (blocks + q) * per_group : (blocks + q + 1) * per_group, :]
                value = value + low.astype(jnp.float32)
            results[q] = results[q] + weight * value
    for q in range(blocks):
        out_ref[:, q * LANES : (q + 1) * LANES] = results[q]


def local(eigvec_rows, split, shifts, roots, deflate_mask, panel_source):
    height, width = eigvec_rows.shape
    row_count = lax.axis_size("row")
    col_count = lax.axis_size("col")
    half_devices = row_count // 2
    panel = roots.shape[0]
    tiles = width // LANES
    vmem = pl.BlockSpec(memory_space=pltpu.VMEM)
    anywhere = pl.BlockSpec(memory_space=pl.ANY)
    limit = lambda mib: pltpu.CompilerParams(vmem_limit_bytes=mib * 2**20)
    in_hbm = lambda x: pltpu.with_memory_space_constraint(x, pltpu.HBM)
    square = lambda x: x.reshape(2, tiles, LANES).swapaxes(0, 1).reshape(2 * tiles, LANES)
    struct = jax.ShapeDtypeStruct
    roots = roots.reshape(1, -1)
    panel_source = panel_source.reshape(1, -1)
    shifts = square(shifts)
    deflate_mask = square(deflate_mask)
    row_struct = struct((SUBLANES, panel), jnp.float32)
    line_struct = lambda kind: struct((tiles, LANES), kind)
    square_struct = lambda kind: struct((panel, LANES), kind)
    lines, own_mask, own_shifts, poles, unit, flags, squares, holder = pl.pallas_call(
        functools.partial(pick_kernel, columns=width * col_count),
        out_shape=(
            struct((half_devices, tiles, LANES), eigvec_rows.dtype),
            line_struct(jnp.int32),
            line_struct(jnp.float32),
            square_struct(jnp.float32),
            square_struct(jnp.int32),
            row_struct,
            struct((panel, width), jnp.float32),
            struct((half_devices, LANES), jnp.float32),
        ),
        in_specs=[anywhere] * 6,
        out_specs=(vmem,) * 8,
        scratch_shapes=[
            pltpu.SMEM((2,), jnp.int32),
            pltpu.VMEM((ALIGN, width), eigvec_rows.dtype),
            pltpu.VMEM((2 * tiles, LANES), jnp.float32),
            pltpu.VMEM((2 * tiles, LANES), jnp.int32),
            pltpu.VMEM((1, panel), jnp.float32),
            pltpu.VMEM((1, panel), jnp.int32),
            pltpu.SemaphoreType.DMA((6,)),
        ],
        compiler_params=limit(4),
        name="pick_line",
    )(*[in_hbm(x) for x in (split, eigvec_rows, shifts, deflate_mask, roots, panel_source)])
    halves = [list(range(half_devices)), list(range(half_devices, row_count))]
    lines = lax.all_to_all(lines, "row", 0, 0, axis_index_groups=halves)
    norm, sums, kept = pl.pallas_call(
        norm_kernel,
        out_shape=(row_struct, row_struct, line_struct(jnp.float32)),
        in_specs=[vmem] * 5,
        out_specs=(vmem,) * 3,
        scratch_shapes=[pltpu.VMEM((tiles, LANES), jnp.float32)],
        compiler_params=limit(8),
        name="column_norms",
    )(holder, lines, own_mask, squares, flags)
    flip = half_devices + half_devices // 2
    other = lax.ppermute(norm, "row", [(i, i ^ flip) for i in range(row_count)])
    body = panel // col_count * (height // LANES + LOW_BLOCKS)
    parts = pl.pallas_call(
        product_kernel,
        out_shape=struct((col_count, body + ALIGN, LANES), jnp.bfloat16),
        in_specs=[vmem] * 5,
        out_specs=vmem,
        compiler_params=limit(16),
        cost_estimate=pl.CostEstimate(flops=2 * 10**9, bytes_accessed=2**24, transcendentals=2**20),
        name="block_product",
    )(kept, own_shifts, poles, unit, eigvec_rows)
    norms = sums + other
    first = lax.reduce_precision(norms, 8, 7)
    extra = jnp.concatenate([first, norms - first]).astype(jnp.bfloat16)
    extra = jnp.broadcast_to(extra, (col_count, ALIGN, LANES))
    parts = lax.dynamic_update_slice(parts, extra, (0, body, 0))
    parts = lax.all_to_all(parts, "col", 0, 0)
    return pl.pallas_call(
        finish_kernel,
        out_shape=struct((panel // col_count, height), jnp.float32),
        in_specs=[vmem],
        out_specs=vmem,
        scratch_shapes=[pltpu.VMEM((panel, col_count), jnp.float32)],
        compiler_params=limit(4),
        name="scale_and_add",
    )(parts)


def solution(mesh):
    return jax.shard_map(
        local,
        mesh=mesh,
        in_specs=(P("row", "col"), P(), P(None, "col"), P(), P(None, "col"), P()),
        out_specs=P("col", "row"),
        check_vma=False,
    )
```

```python
import functools

import jax
import jax.numpy as jnp
from jax import lax
from jax.experimental import pallas as pl
from jax.experimental.pallas import tpu as pltpu
from jax.sharding import PartitionSpec as P

LANES = 128
ALIGN = 16
SUBLANES = 8
CHUNKS = 8
LOW_BLOCKS = 2


def spread(line):
    return jnp.broadcast_to(line, (LANES, line.shape[1])).T


def pick_kernel(
    split_hbm, rows_hbm, shifts_hbm, mask_hbm, roots_hbm, source_hbm,
    out_ref, own_mask_ref, own_shifts_ref, poles_ref, unit_ref, flags_ref, squares_ref, holder_ref,
    split_ref, window, shifts_ref, mask_ref, roots_ref, source_ref, sems, *, columns
):
    half = lax.axis_index("row") // (lax.axis_size("row") // 2)
    height, width = rows_hbm.shape
    panel = roots_ref.shape[1]
    tiles = width // LANES
    pairs = ((mask_hbm, mask_ref), (source_hbm, source_ref), (roots_hbm, roots_ref), (shifts_hbm, shifts_ref))
    split_copy = pltpu.make_async_copy(split_hbm, split_ref, sems.at[0])
    copies = [pltpu.make_async_copy(a, b, sems.at[i + 2]) for i, (a, b) in enumerate(pairs)]
    split_copy.start()
    for copy in copies:
        copy.start()
    split_copy.wait()
    row = split_ref[half] % height
    device = lax.broadcasted_iota(jnp.int32, holder_ref.shape, 0)
    holder_ref[...] = jnp.where(device == split_ref[half] // height, 1.0, 0.0)
    base = pl.multiple_of((row // ALIGN) * ALIGN, ALIGN)
    row_copy = pltpu.make_async_copy(rows_hbm.at[pl.ds(base, ALIGN)], window, sems.at[1])
    row_copy.start()
    for copy in copies:
        copy.wait()
    own_mask_ref[...] = mask_ref[pl.ds(half, tiles, stride=2), :]
    own_shifts_ref[...] = shifts_ref[pl.ds(half, tiles, stride=2), :]
    source = spread(source_ref[...])
    source_half = (source >= columns).astype(jnp.int32)
    local = source - source_half * columns - lax.axis_index("col") * width
    here = (local >= 0) & (local < width)
    lane = lax.broadcasted_iota(jnp.int32, (panel, LANES), 1)
    tile_of = jnp.where(here, local // LANES * 2 + source_half, -1)
    picked = jnp.dot(
        jnp.where(lax.broadcasted_iota(jnp.int32, (panel, 2 * tiles), 1) == tile_of[:, 0:1], 1.0, 0.0).astype(jnp.bfloat16),
        mask_ref[...].astype(jnp.float32).astype(jnp.bfloat16),
        preferred_element_type=jnp.float32,
    )
    deflated = jnp.sum(jnp.where(lane == local % LANES, picked, 0.0), axis=1, keepdims=True) > 0.5
    own_flag = deflated & (source_half == half)
    poles_ref[...] = jnp.where(own_flag, 3e38, spread(roots_ref[...]))
    unit_ref[...] = jnp.where(own_flag, local, -1)
    own = jnp.where(own_flag, 1.0, 0.0)
    other = jnp.where(deflated & (source_half != half), 1.0, 0.0)
    flags_ref[...] = jnp.where(lane == 1, own, jnp.where(lane == 2, other, 0.0)).T[0:SUBLANES]
    roots_all = spread(roots_ref[...])
    for t in range(tiles):
        inverse = pltpu.reciprocal(own_shifts_ref[t : t + 1, :] - roots_all, approx=True)
        squares_ref[:, t * LANES : (t + 1) * LANES] = inverse * inverse
    row_copy.wait()
    inner = row - base
    lower = inner < SUBLANES
    inner = lax.rem(inner, SUBLANES)
    sublane = lax.broadcasted_iota(jnp.int32, (SUBLANES, LANES), 0)
    blocks = [jnp.zeros((SUBLANES, LANES), jnp.float32) for _ in range(tiles // SUBLANES)]
    for t in range(tiles):
        both = window[:, t * LANES : (t + 1) * LANES].astype(jnp.float32)
        eight = jnp.where(lower, both[0:SUBLANES], both[SUBLANES:])
        target = t % SUBLANES
        turned = pltpu.roll(eight, lax.rem(target - inner + SUBLANES, SUBLANES), 0)
        blocks[t // SUBLANES] = jnp.where(sublane == target, turned, blocks[t // SUBLANES])
    line = jnp.concatenate(blocks, axis=0).astype(out_ref.dtype)
    for target in range(out_ref.shape[0]):
        out_ref[target] = line


def norm_kernel(
    holder_ref, lines_ref, mask_ref, squares_ref, flags_ref, norm_ref, sums_ref, kept_ref, line_ref
):
    panel = squares_ref.shape[0]
    tiles = lines_ref.shape[1]
    line = jnp.zeros((tiles, LANES), jnp.float32)
    for device in range(lines_ref.shape[0]):
        line = jnp.where(holder_ref[device : device + 1, :] > 0.5, lines_ref[device].astype(jnp.float32), line)
    kept = jnp.where(mask_ref[...] == 1, 0.0, line)
    kept_ref[...] = kept
    line_ref[...] = kept * kept
    norm = jnp.zeros((panel, LANES), jnp.float32)
    for t in range(tiles):
        norm = norm + line_ref[t : t + 1, :] * squares_ref[:, t * LANES : (t + 1) * LANES]
    lane = lax.broadcasted_iota(jnp.int32, (panel, LANES), 1)
    norm = jnp.where(lane == 0, jnp.sum(norm, axis=1, keepdims=True), 0.0).T[0:1]
    high = norm.astype(jnp.bfloat16).astype(jnp.float32)
    row = lax.broadcasted_iota(jnp.int32, norm_ref.shape, 0)
    norm_ref[...] = jnp.where(row == 3, high, jnp.where(row == 4, norm - high, 0.0)).astype(norm_ref.dtype)
    flags = jnp.concatenate([flags_ref[...], jnp.zeros_like(flags_ref[...])])
    sums_ref[...] = jnp.where(row == 0, high, jnp.where(row == SUBLANES, norm - high, flags)).astype(sums_ref.dtype)


def product_kernel(kept_ref, shifts_ref, poles_ref, unit_ref, rows_ref, out_ref):
    panel = poles_ref.shape[0]
    groups = out_ref.shape[0]
    per_group = panel // groups
    height, width = rows_ref.shape
    poles = poles_ref[...]
    unit = unit_ref[...]
    lane = lax.broadcasted_iota(jnp.int32, (1, LANES), 1)
    total = jnp.zeros((2 * panel, height), jnp.float32)
    chunk = width // CHUNKS
    for c in range(CHUNKS):
        highs, lows = [], []
        for t in range(c * chunk // LANES, (c + 1) * chunk // LANES):
            cauchy = kept_ref[t : t + 1, :] * pltpu.reciprocal(shifts_ref[t : t + 1, :] - poles, approx=True)
            value = jnp.where(unit == lane + t * LANES, 1.0, cauchy)
            high = value.astype(jnp.bfloat16)
            highs.append(high)
            lows.append((value - high.astype(jnp.float32)).astype(jnp.bfloat16))
        merged = jnp.concatenate([jnp.concatenate(highs, axis=1), jnp.concatenate(lows, axis=1)], axis=0)
        total = total + lax.dot_general(
            merged, rows_ref[:, c * chunk : (c + 1) * chunk], (((1,), (1,)), ((), ())),
            preferred_element_type=jnp.float32,
        )
    product = (total[0:panel] + total[panel : 2 * panel]).reshape(groups, per_group, height)
    blocks = height // LANES
    for q in range(blocks):
        block = product[:, :, q * LANES : (q + 1) * LANES]
        high = block.astype(jnp.bfloat16)
        out_ref[:, q * per_group : (q + 1) * per_group, :] = high
        if q < LOW_BLOCKS:
            low = (block - high.astype(jnp.float32)).astype(jnp.bfloat16)
            out_ref[:, (blocks + q) * per_group : (blocks + q + 1) * per_group, :] = low
    extra = (blocks + LOW_BLOCKS) * per_group
    out_ref[:, extra:, :] = jnp.zeros((groups, ALIGN, LANES), jnp.bfloat16)


def finish_kernel(parts_ref, out_ref, columns_ref):
    groups = parts_ref.shape[0]
    per_group, height = out_ref.shape
    blocks = height // LANES
    extra = (blocks + LOW_BLOCKS) * per_group
    rows = parts_ref[:, extra:, :].astype(jnp.float32)
    total = jnp.sum(rows, axis=0)
    norm2 = (total[0:1] + total[3:4]) + (total[4:5] + total[SUBLANES : SUBLANES + 1])
    own, other = total[1:2], total[2:3]
    scale = jnp.where(other > 0.5, 0.0, 1.0 / jnp.sqrt(norm2))
    weights = [jnp.where(own > 0.5, rows[group, 1:2], scale) for group in range(groups)]
    columns_ref[...] = jnp.concatenate(weights, axis=0).T
    start = pl.multiple_of(lax.axis_index("col") * per_group, per_group)
    weights = columns_ref[pl.ds(start, per_group), :]
    results = [jnp.zeros((per_group, LANES), jnp.float32) for _ in range(blocks)]
    for group in range(groups):
        weight = weights[:, group : group + 1]
        for q in range(blocks):
            value = parts_ref[group, q * per_group : (q + 1) * per_group, :].astype(jnp.float32)
            if q < LOW_BLOCKS:
                low = parts_ref[group, (blocks + q) * per_group : (blocks + q + 1) * per_group, :]
                value = value + low.astype(jnp.float32)
            results[q] = results[q] + weight * value
    for q in range(blocks):
        out_ref[:, q * LANES : (q + 1) * LANES] = results[q]


def local(eigvec_rows, split, shifts, roots, deflate_mask, panel_source):
    height, width = eigvec_rows.shape
    row_count = lax.axis_size("row")
    col_count = lax.axis_size("col")
    half_devices = row_count // 2
    panel = roots.shape[0]
    tiles = width // LANES
    vmem = pl.BlockSpec(memory_space=pltpu.VMEM)
    anywhere = pl.BlockSpec(memory_space=pl.ANY)
    limit = lambda mib: pltpu.CompilerParams(vmem_limit_bytes=mib * 2**20)
    in_hbm = lambda x: pltpu.with_memory_space_constraint(x, pltpu.HBM)
    square = lambda x: x.reshape(2, tiles, LANES).swapaxes(0, 1).reshape(2 * tiles, LANES)
    struct = jax.ShapeDtypeStruct
    roots = roots.reshape(1, -1)
    panel_source = panel_source.reshape(1, -1)
    shifts = square(shifts)
    deflate_mask = square(deflate_mask)
    row_struct = struct((SUBLANES, panel), jnp.float32)
    line_struct = lambda kind: struct((tiles, LANES), kind)
    square_struct = lambda kind: struct((panel, LANES), kind)
    lines, own_mask, own_shifts, poles, unit, flags, squares, holder = pl.pallas_call(
        functools.partial(pick_kernel, columns=width * col_count),
        out_shape=(
            struct((half_devices, tiles, LANES), eigvec_rows.dtype),
            line_struct(jnp.int32),
            line_struct(jnp.float32),
            square_struct(jnp.float32),
            square_struct(jnp.int32),
            row_struct,
            struct((panel, width), jnp.float32),
            struct((half_devices, LANES), jnp.float32),
        ),
        in_specs=[anywhere] * 6,
        out_specs=(vmem,) * 8,
        scratch_shapes=[
            pltpu.SMEM((2,), jnp.int32),
            pltpu.VMEM((ALIGN, width), eigvec_rows.dtype),
            pltpu.VMEM((2 * tiles, LANES), jnp.float32),
            pltpu.VMEM((2 * tiles, LANES), jnp.int32),
            pltpu.VMEM((1, panel), jnp.float32),
            pltpu.VMEM((1, panel), jnp.int32),
            pltpu.SemaphoreType.DMA((6,)),
        ],
        compiler_params=limit(4),
        name="pick_line",
    )(*[in_hbm(x) for x in (split, eigvec_rows, shifts, deflate_mask, roots, panel_source)])
    halves = [list(range(half_devices)), list(range(half_devices, row_count))]
    lines = lax.all_to_all(lines, "row", 0, 0, axis_index_groups=halves)
    norm, sums, kept = pl.pallas_call(
        norm_kernel,
        out_shape=(struct((ALIGN, panel), jnp.bfloat16),) * 2 + (line_struct(jnp.float32),),
        in_specs=[vmem] * 5,
        out_specs=(vmem,) * 3,
        scratch_shapes=[pltpu.VMEM((tiles, LANES), jnp.float32)],
        compiler_params=limit(8),
        name="column_norms",
    )(holder, lines, own_mask, squares, flags)
    flip = half_devices + half_devices // 2
    other = lax.ppermute(norm, "row", [(i, i ^ flip) for i in range(row_count)])
    body = panel // col_count * (height // LANES + LOW_BLOCKS)
    parts = pl.pallas_call(
        product_kernel,
        out_shape=struct((col_count, body + ALIGN, LANES), jnp.bfloat16),
        in_specs=[vmem] * 5,
        out_specs=vmem,
        compiler_params=limit(16),
        cost_estimate=pl.CostEstimate(flops=2 * 10**9, bytes_accessed=2**24, transcendentals=2**20),
        name="block_product",
    )(kept, own_shifts, poles, unit, eigvec_rows)
    extra = jnp.broadcast_to(sums + other, (col_count, ALIGN, LANES))
    parts = lax.dynamic_update_slice(parts, extra, (0, body, 0))
    parts = lax.all_to_all(parts, "col", 0, 0)
    return pl.pallas_call(
        finish_kernel,
        out_shape=struct((panel // col_count, height), jnp.float32),
        in_specs=[vmem],
        out_specs=vmem,
        scratch_shapes=[pltpu.VMEM((panel, col_count), jnp.float32)],
        compiler_params=limit(4),
        name="scale_and_add",
    )(parts)


def solution(mesh):
    return jax.shard_map(
        local,
        mesh=mesh,
        in_specs=(P("row", "col"), P(), P(None, "col"), P(), P(None, "col"), P()),
        out_specs=P("col", "row"),
        check_vma=False,
    )
```
